128 devices in a mesh: gx: 4 (over y_hi, core), gy: 4 (over x), gz: 8 (over z, y_lo).
Axes of the slice: x: 4, y: 4 (y_hi: 2, y_lo: 2; y = y_hi * 2 + y_lo), z: 4, core: 2. Of those that a mesh axis runs over, the one named last changes fastest.
Arguments:
- terminal_adjoint: float32 [19, 64, 128, 1024], P(None, 'gx', 'gy', 'gz'), may hold values from -6 to 6
- saved_velocity: float32 [4, 3, 64, 128, 1024], P(None, None, 'gx', 'gy', 'gz'), may hold values from -0.15 to 0.15
- solid_mask: int32 [64, 128, 1024], P('gx', 'gy', 'gz'), may hold values 0 or 1
- wall_ids: int32 [64, 128, 1024], P('gx', 'gy', 'gz'), may hold values from 0 to 255
Outputs:
- adjoint_out: float32 [19, 64, 128, 1024], P(None, 'gx', 'gy', 'gz')
- wall_grad: float32 [4, 128], replicated
The draws below stay inside these ranges and needn't reach their ends.
Inputs may be any that keep to these rules, and one draw needn't show every extreme that they name: `wall_ids`: ids of 128 or more mark cells on no wall panel.
All inputs are finite; a program needn't handle non-finite values. No bound on the sum of `solid_mask` on one device may be relied on, other than what follows from the above.
Results may differ from the reference program's by a relative error of at most 0.0003.
Values sent between devices are 32-bit elements; how exact they have to be, the bound alone decides.
A program may use at most 128 MiB of HBM per device.

```python
import jax
import jax.numpy as jnp

STEPS = 4
WALLS = 128
NX = 64
NY = 128
NZ = 1024


def set_ends(drawn, rng, low, largest):
    dims = drawn.shape
    index_at = [jax.random.randint(jax.random.fold_in(rng, axis), (), 0, dims[axis]) for axis in range(len(dims))]
    drawn = drawn.at[tuple(index_at)].set(low)
    longest = dims.index(max(dims))
    index_at[longest] = (index_at[longest] + 1) % dims[longest]
    return drawn.at[tuple(index_at)].set(largest)


def shard_levels(key, dims, cuts, low, top_value):
    def one(position, blocks):
        heights = jax.random.uniform(jax.random.fold_in(jax.random.fold_in(key, 6), position), (blocks,), jnp.float32, low / len(cuts), top_value / len(cuts))
        return jnp.repeat(jnp.exp(heights), dims[position] // blocks).reshape((-1,) + (1,) * (len(dims) - position - 1))

    gain = one(*cuts[0])
    for cut in cuts[1:]:
        gain = gain * one(*cut)
    return gain


def scatter_about(own_key, shape, spread, bound, shards=(), kind=jnp.bfloat16):
    values = jax.random.normal(own_key, shape, jnp.float32) * spread
    if len(shards) > 0:
        values = shard_levels(own_key, shape, shards, -0.22, 0.18) * values
    return jnp.clip(values, min=-bound, max=bound).astype(kind)


def setup_inputs(seed: int = 0) -> dict:
    splits = jax.random.split(jax.random.key(seed), 5)
    return {
        "terminal_adjoint": scatter_about(splits[0], (19, NX, NY, NZ), 1.0, 6.0, ((1, 4), (2, 4), (3, 8)), jnp.float32),
        "saved_velocity": jnp.clip(jax.random.uniform(splits[1], (STEPS, 3, NX, NY, NZ), jnp.float32, -0.15, 0.15) * shard_levels(splits[1], (STEPS, 3, NX, NY, NZ), ((2, 4), (3, 4), (4, 8)), -0.4, 0.0), -0.15, 0.15),
        "solid_mask": set_ends((jax.random.randint(splits[2], (NX, NY, NZ), 0, 8) < 1).astype(jnp.int32), jax.random.fold_in(splits[2], 1), 0, 1),
        "wall_ids": set_ends(jax.random.randint(splits[3], (NX, NY, NZ), 0, 2 * WALLS), jax.random.fold_in(splits[3], 1), 0, (2 * WALLS) - 1).astype(jnp.int32),
    }


LATTICE = ((0, 0, 0), (1, 0, 0), (-1, 0, 0), (0, 1, 0), (0, -1, 0), (0, 0, 1), (0, 0, -1),
           (1, 1, 0), (-1, -1, 0), (1, -1, 0), (-1, 1, 0), (1, 0, 1), (-1, 0, -1),
           (1, 0, -1), (-1, 0, 1), (0, 1, 1), (0, -1, -1), (0, 1, -1), (0, -1, 1))
OPPOSITE = (0, 2, 1, 4, 3, 6, 5, 8, 7, 10, 9, 12, 11, 14, 13, 16, 15, 18, 17)
WEIGHTS = (1.0 / 3.0,) + (1.0 / 18.0,) * 6 + (1.0 / 36.0,) * 12
OMEGA = 1.25


def pull_fields(padded, shape):
    fields = []
    for member in range(19):
        vector = LATTICE[member]
        fields.append(padded[member, 1 + vector[0]:1 + vector[0] + shape[0],
                             1 + vector[1]:1 + vector[1] + shape[1],
                             1 + vector[2]:1 + vector[2] + shape[2]])
    return jnp.stack(fields)


def collide_back(read, velocity, solid):
    speed_sq = velocity[0] * velocity[0] + velocity[1] * velocity[1] + velocity[2] * velocity[2]
    scalar_sum = jnp.zeros_like(speed_sq)
    grads = [jnp.zeros_like(speed_sq) for spatial in range(3)]
    for member in range(19):
        vector = LATTICE[member]
        along = vector[0] * velocity[0] + vector[1] * velocity[1] + vector[2] * velocity[2]
        weighted = WEIGHTS[member] * read[member]
        scalar_sum = scalar_sum + weighted * (1.0 + 3.0 * along + 4.5 * along * along - 1.5 * speed_sq)
        for spatial in range(3):
            grads[spatial] = grads[spatial] + weighted * (3.0 * vector[spatial] + 9.0 * along * vector[spatial] - 3.0 * velocity[spatial])
    outputs = []
    for member in range(19):
        vector = LATTICE[member]
        coupled = scalar_sum
        for spatial in range(3):
            coupled = coupled + grads[spatial] * (vector[spatial] - velocity[spatial])
        fluid = (1.0 - OMEGA) * read[member] + OMEGA * coupled
        outputs.append(jnp.where(solid == 1, read[OPPOSITE[member]], fluid))
    return jnp.stack(outputs)


def pressure_of(adjoint):
    total = jnp.zeros_like(adjoint[0])
    for member in range(19):
        if LATTICE[member][2] != 0:
            total = total + LATTICE[member][2] * adjoint[member]
    return total


def reference(terminal_adjoint, saved_velocity, solid_mask, wall_ids):
    shape = terminal_adjoint.shape[1:]
    count = shape[0] * shape[1] * shape[2] / (2.0 * WALLS)
    scale = count ** -0.5
    adjoint = terminal_adjoint
    rows = [None] * STEPS
    for step in range(STEPS - 1, -1, -1):
        padded = jnp.pad(adjoint, ((0, 0), (1, 1), (1, 1), (1, 1)))
        read = pull_fields(padded, shape)
        adjoint = collide_back(read, saved_velocity[step], solid_mask)
        pressure = pressure_of(adjoint)
        sums = jax.ops.segment_sum(pressure.reshape(-1), wall_ids.reshape(-1).astype(jnp.int32), num_segments=2 * WALLS)
        rows[step] = sums[:WALLS] * scale
    return adjoint, jnp.stack(rows)
```

```python
import functools

import jax
import jax.numpy as jnp
from jax import lax
from jax.experimental import pallas as pl
from jax.experimental.pallas import tpu as pltpu
from jax.sharding import PartitionSpec as P

STEPS = 4
WALLS = 128
OMEGA = 1.25
LATTICE = (
    (0, 0, 0),
    (1, 0, 0),
    (-1, 0, 0),
    (0, 1, 0),
    (0, -1, 0),
    (0, 0, 1),
    (0, 0, -1),
    (1, 1, 0),
    (-1, -1, 0),
    (1, -1, 0),
    (-1, 1, 0),
    (1, 0, 1),
    (-1, 0, -1),
    (1, 0, -1),
    (-1, 0, 1),
    (0, 1, 1),
    (0, -1, -1),
    (0, 1, -1),
    (0, -1, 1),
)
OPPOSITE = (0, 2, 1, 4, 3, 6, 5, 8, 7, 10, 9, 12, 11, 14, 13, 16, 15, 18, 17)

NX, NY, NZ = 16, 32, 128
ROW0 = 8
ROWS = 48
GROUPS = NY // 8

SLOT = {9: 16, 1: 1, 11: 2, 13: 3, 7: 4, 3: 5, 15: 6, 17: 7, 10: 8, 2: 9,
        12: 10, 14: 11, 8: 12, 4: 13, 16: 14, 18: 15, 5: 17, 6: 18, 0: 19}
SLOTS = 20
Y_MEMBERS = ((7, 3, 15, 17, 10), (8, 4, 16, 18, 9))
Z_MEMBERS = ((5, 11, 14, 15, 18), (6, 12, 13, 16, 17))
LANES = NX + 2
MESH = pl.DeviceIdType.MESH


def kernel(
    sizes, adj_ref, vel_ref, solid_ref, ids_ref, out_ref, wall_ref,
    state, vel, solid, ids, ysend, yrecv, zsend, zrecv, xyrecv, xzrecv, yzrecv,
    lo_hot, hi_part, acc, in_sem, out_sem, send_sem, recv_sem,
):
    me = (lax.axis_index("gx"), lax.axis_index("gy"), lax.axis_index("gz"))

    loads = []
    for m in range(19):
        loads.append(
            pltpu.make_async_copy(
                adj_ref.at[m],
                state.at[0, SLOT[m], pl.ds(1, NX), pl.ds(ROW0, NY), :],
                in_sem.at[m],
            )
        )
    loads.append(pltpu.make_async_copy(ids_ref, ids, in_sem.at[19]))
    loads.append(pltpu.make_async_copy(solid_ref, solid, in_sem.at[20]))
    loads.append(pltpu.make_async_copy(vel_ref, vel, in_sem.at[21]))
    for load in loads:
        load.start()

    zero_plane = jnp.zeros((SLOTS, ROWS, NZ), jnp.float32)
    for b in range(2):
        state[b, :, 0] = zero_plane
        state[b, :, NX + 1] = zero_plane
    yrecv[...] = jnp.zeros_like(yrecv)
    zrecv[...] = jnp.zeros_like(zrecv)
    xyrecv[...] = jnp.zeros_like(xyrecv)
    xzrecv[...] = jnp.zeros_like(xzrecv)
    yzrecv[...] = jnp.zeros_like(yzrecv)

    def beside(vector, sign):
        at = tuple(me[k] + sign * vector[k] for k in range(3))
        inside = None
        for k in range(3):
            if vector[k] != 0:
                here = (at[k] >= 0) & (at[k] < sizes[k])
                inside = here if inside is None else inside & here
        return at, inside

    barrier = pltpu.get_barrier_semaphore()
    count = jnp.int32(0)
    for m in range(1, 19):
        at, inside = beside(LATTICE[m], 1)
        count = count + inside.astype(jnp.int32)

        @pl.when(inside)
        def _():
            pl.semaphore_signal(barrier, inc=1, device_id=at, device_id_type=MESH)

    pl.semaphore_wait(barrier, count)

    lane = lax.broadcasted_iota(jnp.int32, (8, NZ), 1)

    def rows_of(group, shift=0):
        return pl.ds(ROW0 + 8 * group + shift, 8)

    loads[19].wait()
    low_iota = lax.broadcasted_iota(jnp.int32, (16, NZ), 0)

    def hot_plane(x, carry):
        for group in range(GROUPS):
            low = ids[x, pl.ds(8 * group, 8), :] & 15
            for y in range(8):
                hot = jnp.broadcast_to(low[y : y + 1, :], (16, NZ)) == low_iota
                lo_hot[x, pl.ds(16 * y, 16), pl.ds(NZ * group, NZ)] = jnp.where(
                    hot, 1.0, 0.0
                ).astype(jnp.bfloat16)
        return carry

    lax.fori_loop(0, NX, hot_plane, 0)

    def pack(b, x, group, values):
        for side in range(2):
            rows = pl.ds(8 * group, 8)
            packed = zsend[b, side, rows, :]
            for i, m in enumerate(Z_MEMBERS[side]):
                place = i * LANES + x + 1
                moved = pltpu.roll(values[m], place + side, 1)
                packed = jnp.where(lane == place, moved, packed)
            zsend[b, side, rows, :] = packed
        if group == 0:
            for i, m in enumerate(Y_MEMBERS[0]):
                ysend[b, 0, i, pl.ds(x, 1), :] = values[m][0:1, :]
        if group == GROUPS - 1:
            for i, m in enumerate(Y_MEMBERS[1]):
                ysend[b, 1, i, pl.ds(x, 1), :] = values[m][7:8, :]

    for m in range(19):
        loads[m].wait()

    def first_pack(x, carry):
        for group in range(GROUPS):
            values = {}
            for m in sorted(set(Y_MEMBERS[0] + Y_MEMBERS[1] + Z_MEMBERS[0] + Z_MEMBERS[1])):
                values[m] = state[0, SLOT[m], x + 1, rows_of(group), :]
            pack(0, x, group, values)
        return carry

    lax.fori_loop(0, NX, first_pack, 0)
    state[0, 0, 1, pl.ds(ROW0, NY), :] = state[0, SLOT[9], 1, pl.ds(ROW0, NY), :]
    loads[20].wait()
    loads[21].wait()

    def message(b, m):
        cells = pl.ds(ROW0, NY)
        if m == 1:
            return state.at[b, pl.ds(0, 5), 1, cells, :], state.at[b, pl.ds(0, 5), NX + 1, cells, :]
        if m == 2:
            return state.at[b, pl.ds(8, 5), NX, cells, :], state.at[b, pl.ds(8, 5), 0, cells, :]
        if m in (3, 4):
            return ysend.at[b, m - 3], yrecv.at[b, m - 3]
        if m in (5, 6):
            return zsend.at[b, m - 5], zrecv.at[b, m - 5, cells, :]
        vector = LATTICE[m]
        if m <= 10:
            side = 0 if vector[1] > 0 else 1
            start = 0 if vector[0] > 0 else NX - 8
            member = Y_MEMBERS[side].index(m)
            return ysend.at[b, side, member, pl.ds(start, 8), :], xyrecv.at[b, m - 7]
        side = 0 if vector[2] > 0 else 1
        if m <= 14:
            return zsend.at[b, side], xzrecv.at[b, m - 11]
        start = 0 if vector[1] > 0 else NY - 8
        return zsend.at[b, side, pl.ds(start, 8), :], yzrecv.at[b, m - 15]

    def copy_of(t, b, m, target):
        source, landing = message(b, m)
        return pltpu.make_async_remote_copy(
            src_ref=source,
            dst_ref=landing,
            send_sem=send_sem.at[t, m - 1],
            recv_sem=recv_sem.at[t, m - 1],
            device_id=target,
            device_id_type=MESH,
        )

    def exchange(t, b):
        for m in range(1, 19):
            at, inside = beside(LATTICE[m], -1)

            @pl.when(inside)
            def _():
                copy_of(t, b, m, at).start()

        for m in range(1, 19):
            at, inside = beside(LATTICE[m], 1)

            @pl.when(inside)
            def _():
                copy_of(t, b, m, at).wait_recv()

        for m in range(1, 19):
            at, inside = beside(LATTICE[m], -1)

            @pl.when(inside)
            def _():
                copy_of(t, b, m, at).wait_send()

    def unpack(b):
        state[b, SLOT[9], NX + 1, pl.ds(ROW0, NY), :] = state[b, 0, NX + 1, pl.ds(ROW0, NY), :]
        for side in range(2):
            row = ROW0 + NY if side == 0 else ROW0 - 1
            for i, m in enumerate(Y_MEMBERS[side]):
                for x in range(NX):
                    state[b, SLOT[m], x + 1, pl.ds(row, 1), :] = yrecv[b, side, i, pl.ds(x, 1), :]
        for m in range(7, 11):
            vector = LATTICE[m]
            plane = NX + 1 if vector[0] > 0 else 0
            row = ROW0 + NY if vector[1] > 0 else ROW0 - 1
            source = 0 if vector[0] > 0 else 7
            state[b, SLOT[m], plane, pl.ds(row, 1), :] = xyrecv[b, m - 7, pl.ds(source, 1), :]
        for m in range(11, 15):
            vector = LATTICE[m]
            side = 0 if vector[2] > 0 else 1
            i = Z_MEMBERS[side].index(m)
            source = i * LANES + (1 if vector[0] > 0 else NX)
            place = i * LANES + (NX + 1 if vector[0] > 0 else 0)
            for group in range(GROUPS):
                moved = pltpu.roll(
                    xzrecv[b, m - 11, pl.ds(8 * group, 8), :], (place - source) % NZ, 1
                )
                zrecv[b, side, rows_of(group), :] = jnp.where(
                    lane == place, moved, zrecv[b, side, rows_of(group), :]
                )
        for m in range(15, 19):
            vector = LATTICE[m]
            side = 0 if vector[2] > 0 else 1
            row = ROW0 + NY if vector[1] > 0 else ROW0 - 1
            source = 0 if vector[1] > 0 else 7
            zrecv[b, side, pl.ds(row, 1), :] = yzrecv[b, m - 15, pl.ds(source, 1), :]

    def pull(b, x, group):
        read = []
        for m in range(19):
            vector = LATTICE[m]
            value = state[b, SLOT[m], x + 1 + vector[0], rows_of(group, vector[1]), :]
            if vector[2] != 0:
                side = 0 if vector[2] > 0 else 1
                place = Z_MEMBERS[side].index(m) * LANES + x + 1 + vector[0]
                column = zrecv[b, side, rows_of(group, vector[1]), :]
                if side == 0:
                    value = jnp.where(
                        lane == NZ - 1,
                        pltpu.roll(column, NZ - 1 - place, 1),
                        pltpu.roll(value, NZ - 1, 1),
                    )
                else:
                    value = jnp.where(
                        lane == 0,
                        pltpu.roll(column, NZ - place, 1),
                        pltpu.roll(value, 1, 1),
                    )
            read.append(value)
        return read

    def collide(read, u, is_solid):
        face_sum = [read[1] + read[2], read[3] + read[4], read[5] + read[6]]
        face_dif = [read[1] - read[2], read[3] - read[4], read[5] - read[6]]
        sums, twist, first, second = [], [], [], []
        for m in (7, 11, 15):
            plus, minus = read[m] + read[m + 1], read[m + 2] + read[m + 3]
            dplus, dminus = read[m] - read[m + 1], read[m + 2] - read[m + 3]
            sums.append(plus + minus)
            twist.append(plus - minus)
            first.append(dplus + dminus)
            second.append(dplus - dminus)
        xy, xz, yz = 0, 1, 2
        twice = [value + value for value in face_sum]
        rho = 12.0 * read[0] + (twice[0] + twice[1] + twice[2]) + (sums[xy] + sums[xz] + sums[yz])
        edge = [first[xy] + first[xz], second[xy] + first[yz], second[xz] + second[yz]]
        flux = [(face_dif[k] + face_dif[k]) + edge[k] for k in range(3)]
        stress = [
            twice[0] + (sums[xy] + sums[xz]),
            twice[1] + (sums[xy] + sums[yz]),
            twice[2] + (sums[xz] + sums[yz]),
        ]
        u3 = [3.0 * value for value in u]
        w = [
            rho * u[0] - (stress[0] * u3[0] + twist[xy] * u3[1] + twist[xz] * u3[2]),
            rho * u[1] - (twist[xy] * u3[0] + stress[1] * u3[1] + twist[yz] * u3[2]),
            rho * u[2] - (twist[xz] * u3[0] + twist[yz] * u3[1] + stress[2] * u3[2]),
        ]
        g = [(OMEGA * 3.0 / 36.0) * (flux[k] - w[k]) for k in range(3)]
        base = (OMEGA / 36.0) * rho + (OMEGA * 1.5 / 36.0) * (u[0] * w[0] + u[1] * w[1] + u[2] * w[2])
        along = [None] * 19
        along[0] = base
        for k in range(3):
            along[1 + 2 * k] = base + g[k]
            along[2 + 2 * k] = base - g[k]
        for m, (j, k) in ((7, (0, 1)), (11, (0, 2)), (15, (1, 2))):
            total, difference = g[j] + g[k], g[j] - g[k]
            along[m], along[m + 1] = base + total, base - total
            along[m + 2], along[m + 3] = base + difference, base - difference
        outputs = [
            jnp.where(is_solid, read[OPPOSITE[m]], along[m] + (1.0 - OMEGA) * read[m])
            for m in range(19)
        ]
        momentum = face_dif[2] + edge[2]
        pressure = jnp.where(is_solid, -momentum, 10.0 * g[2] + (1.0 - OMEGA) * momentum)
        return outputs, pressure

    out_row = lax.broadcasted_iota(jnp.int32, (128, NZ), 0)
    out_lane = lax.broadcasted_iota(jnp.int32, (128, NZ), 1)
    same_y = (out_row & 7) == (out_lane >> 4)
    own_lane = lax.broadcasted_iota(jnp.int32, (8, NZ), 0) == (lane >> 4)

    def one_step(t, carry):
        b = lax.rem(t, 2)
        nb = 1 - b
        exchange(t, b)
        unpack(b)
        acc[...] = jnp.zeros_like(acc)

        def one_plane(x, inner):
            for group in range(GROUPS):
                rows = pl.ds(8 * group, 8)
                read = pull(b, x, group)
                u = [vel[STEPS - 1 - t, k, x, rows, :] for k in range(3)]
                outputs, pressure = collide(read, u, solid[x, rows, :] == 1)
                for m in range(19):
                    state[nb, SLOT[m], x + 1, rows_of(group), :] = outputs[m]
                pack(nb, x, group, outputs)
                upper = pressure.astype(jnp.bfloat16).astype(jnp.float32)
                both = jnp.concatenate([upper, pressure - upper], axis=0).astype(jnp.bfloat16)
                high = (ids[x, rows, :] >> 4).astype(jnp.float32)
                high = jnp.concatenate([high, high], axis=0).astype(jnp.bfloat16)
                for h in range(8):
                    hi_part[pl.ds(16 * h, 16), pl.ds(NZ * group, NZ)] = jnp.where(
                        high == h, both, jnp.zeros_like(both)
                    )
            acc[...] += lax.dot_general(
                hi_part[...],
                lo_hot[x],
                (((1,), (1,)), ((), ())),
                preferred_element_type=jnp.float32,
            )
            return inner

        lax.fori_loop(0, NX, one_plane, 0)
        state[nb, 0, 1, pl.ds(ROW0, NY), :] = state[nb, SLOT[9], 1, pl.ds(ROW0, NY), :]

        own = jnp.where(same_y, acc[...], 0.0)
        total = jnp.sum(own.reshape(8, 16, NZ), axis=1)
        for shift in (64, 32, 16):
            total = total + pltpu.roll(total, shift, 1)
        wall_ref[pl.ds(STEPS - 1 - t, 1), :] = jnp.sum(
            jnp.where(own_lane, total, 0.0), axis=0, keepdims=True
        )
        return carry

    lax.fori_loop(0, STEPS, one_step, 0)

    stores = []
    for m in range(19):
        stores.append(
            pltpu.make_async_copy(
                state.at[STEPS % 2, SLOT[m], pl.ds(1, NX), pl.ds(ROW0, NY), :],
                out_ref.at[m],
                out_sem.at[m],
            )
        )
    for store in stores:
        store.start()
    for store in stores:
        store.wait()


def body(terminal_adjoint, saved_velocity, solid_mask, wall_ids):
    sizes = tuple(lax.axis_size(name) for name in ("gx", "gy", "gz"))
    cells_all = NX * NY * NZ * sizes[0] * sizes[1] * sizes[2]
    scale = (cells_all / (2.0 * WALLS)) ** (-0.5)
    f32, vmem = jnp.float32, pltpu.VMEM
    adjoint, local = pl.pallas_call(
        functools.partial(kernel, sizes),
        out_shape=(
            jax.ShapeDtypeStruct((19, NX, NY, NZ), f32),
            jax.ShapeDtypeStruct((STEPS, WALLS), f32),
        ),
        in_specs=[pl.BlockSpec(memory_space=pl.ANY)] * 4,
        out_specs=(pl.BlockSpec(memory_space=pl.ANY), pl.BlockSpec(memory_space=pltpu.VMEM)),
        scratch_shapes=[
            vmem((2, SLOTS, NX + 2, ROWS, NZ), f32),
            vmem((STEPS, 3, NX, NY, NZ), f32),
            vmem((NX, NY, NZ), jnp.int32),
            vmem((NX, NY, NZ), jnp.int32),
            vmem((2, 2, 5, NX, NZ), f32),
            vmem((2, 2, 5, NX, NZ), f32),
            vmem((2, 2, NY, NZ), f32),
            vmem((2, 2, ROWS, NZ), f32),
            vmem((2, 4, 8, NZ), f32),
            vmem((2, 4, NY, NZ), f32),
            vmem((2, 4, 8, NZ), f32),
            vmem((NX, 128, GROUPS * NZ), jnp.bfloat16),
            vmem((128, GROUPS * NZ), jnp.bfloat16),
            vmem((128, NZ), f32),
            pltpu.SemaphoreType.DMA((22,)),
            pltpu.SemaphoreType.DMA((19,)),
            pltpu.SemaphoreType.DMA((STEPS, 18)),
            pltpu.SemaphoreType.DMA((STEPS, 18)),
        ],
        compiler_params=pltpu.CompilerParams(
            collective_id=0, has_side_effects=True, vmem_limit_bytes=48 * 2**20
        ),
        name="adjoint_steps",
    )(terminal_adjoint, saved_velocity, solid_mask, wall_ids)
    wall_grad = lax.psum(local, ("gx", "gy", "gz")) * scale
    return (adjoint, wall_grad)


def solution(mesh):
    return jax.shard_map(
        body,
        mesh=mesh,
        in_specs=(
            P(None, "gx", "gy", "gz"),
            P(None, None, "gx", "gy", "gz"),
            P("gx", "gy", "gz"),
            P("gx", "gy", "gz"),
        ),
        out_specs=(P(None, "gx", "gy", "gz"), P()),
        check_vma=False,
    )
```

```python
import functools

import jax
import jax.numpy as jnp
from jax import lax
from jax.experimental import pallas as pl
from jax.experimental.pallas import tpu as pltpu
from jax.sharding import PartitionSpec as P

STEPS = 4
WALLS = 128
OMEGA = 1.25
LATTICE = (
    (0, 0, 0),
    (1, 0, 0),
    (-1, 0, 0),
    (0, 1, 0),
    (0, -1, 0),
    (0, 0, 1),
    (0, 0, -1),
    (1, 1, 0),
    (-1, -1, 0),
    (1, -1, 0),
    (-1, 1, 0),
    (1, 0, 1),
    (-1, 0, -1),
    (1, 0, -1),
    (-1, 0, 1),
    (0, 1, 1),
    (0, -1, -1),
    (0, 1, -1),
    (0, -1, 1),
)
OPPOSITE = (0, 2, 1, 4, 3, 6, 5, 8, 7, 10, 9, 12, 11, 14, 13, 16, 15, 18, 17)

NX, NY, NZ = 16, 32, 128
ROW0 = 8
ROWS = 48
GROUPS = NY // 8

SLOT = {9: 16, 1: 1, 11: 2, 13: 3, 7: 4, 3: 5, 15: 6, 17: 7, 10: 8, 2: 9,
        12: 10, 14: 11, 8: 12, 4: 13, 16: 14, 18: 15, 5: 17, 6: 18, 0: 19}
SLOTS = 20
Y_MEMBERS = ((7, 3, 15, 17, 10), (8, 4, 16, 18, 9))
Z_MEMBERS = ((5, 11, 14, 15, 18), (6, 12, 13, 16, 17))
LANES = NX + 2
MESH = pl.DeviceIdType.MESH


def kernel(
    sizes, adj_ref, vel_ref, solid_ref, ids_ref, out_ref, wall_ref,
    state, vel, solid, ids, ysend, yrecv, zsend, zrecv, xyrecv, xzrecv, yzrecv,
    lo_hot, hi_part, acc, sums, wall_xy, wall_z,
    in_sem, out_sem, send_sem, recv_sem, xy_sem, z_sem,
):
    me = (lax.axis_index("gx"), lax.axis_index("gy"), lax.axis_index("gz"))

    loads = []
    for m in range(19):
        loads.append(
            pltpu.make_async_copy(
                adj_ref.at[m],
                state.at[0, SLOT[m], pl.ds(1, NX), pl.ds(ROW0, NY), :],
                in_sem.at[m],
            )
        )
    loads.append(pltpu.make_async_copy(ids_ref, ids, in_sem.at[19]))
    loads.append(pltpu.make_async_copy(solid_ref, solid, in_sem.at[20]))
    loads.append(pltpu.make_async_copy(vel_ref, vel, in_sem.at[21]))
    for load in loads:
        load.start()

    zero_plane = jnp.zeros((SLOTS, ROWS, NZ), jnp.float32)
    for b in range(2):
        state[b, :, 0] = zero_plane
        state[b, :, NX + 1] = zero_plane
    yrecv[...] = jnp.zeros_like(yrecv)
    zrecv[...] = jnp.zeros_like(zrecv)
    xyrecv[...] = jnp.zeros_like(xyrecv)
    xzrecv[...] = jnp.zeros_like(xzrecv)
    yzrecv[...] = jnp.zeros_like(yzrecv)

    def beside(vector, sign):
        at = tuple(me[k] + sign * vector[k] for k in range(3))
        inside = None
        for k in range(3):
            if vector[k] != 0:
                here = (at[k] >= 0) & (at[k] < sizes[k])
                inside = here if inside is None else inside & here
        return at, inside

    barrier = pltpu.get_barrier_semaphore()
    count = jnp.int32(0)
    for m in range(1, 19):
        at, inside = beside(LATTICE[m], 1)
        count = count + inside.astype(jnp.int32)

        @pl.when(inside)
        def _():
            pl.semaphore_signal(barrier, inc=1, device_id=at, device_id_type=MESH)

    plane = sizes[0] * sizes[1]
    xy_others, z_others = [], []
    for k in range(1, plane):
        there = lax.rem(me[0] * sizes[1] + me[1] + k, plane)
        xy_others.append((there // sizes[1], lax.rem(there, sizes[1]), me[2]))
    for k in range(1, sizes[2]):
        z_others.append((me[0], me[1], lax.rem(me[2] + k, sizes[2])))
    for target in xy_others + z_others:
        pl.semaphore_signal(barrier, inc=1, device_id=target, device_id_type=MESH)
    pl.semaphore_wait(barrier, count + len(xy_others) + len(z_others))

    lane = lax.broadcasted_iota(jnp.int32, (8, NZ), 1)

    def rows_of(group, shift=0):
        return pl.ds(ROW0 + 8 * group + shift, 8)

    loads[19].wait()
    low_iota = lax.broadcasted_iota(jnp.int32, (16, NZ), 0)

    def hot_plane(x, carry):
        for group in range(GROUPS):
            low = ids[x, pl.ds(8 * group, 8), :] & 15
            for y in range(8):
                hot = jnp.broadcast_to(low[y : y + 1, :], (16, NZ)) == low_iota
                lo_hot[x, pl.ds(16 * y, 16), pl.ds(NZ * group, NZ)] = jnp.where(
                    hot, 1.0, 0.0
                ).astype(jnp.bfloat16)
        return carry

    lax.fori_loop(0, NX, hot_plane, 0)

    def pack(b, x, group, values):
        for side in range(2):
            rows = pl.ds(8 * group, 8)
            packed = zsend[b, side, rows, :]
            for i, m in enumerate(Z_MEMBERS[side]):
                place = i * LANES + x + 1
                moved = pltpu.roll(values[m], place + side, 1)
                packed = jnp.where(lane == place, moved, packed)
            zsend[b, side, rows, :] = packed
        if group == 0:
            for i, m in enumerate(Y_MEMBERS[0]):
                ysend[b, 0, i, pl.ds(x, 1), :] = values[m][0:1, :]
        if group == GROUPS - 1:
            for i, m in enumerate(Y_MEMBERS[1]):
                ysend[b, 1, i, pl.ds(x, 1), :] = values[m][7:8, :]

    for m in range(19):
        loads[m].wait()

    def first_pack(x, carry):
        for group in range(GROUPS):
            values = {}
            for m in sorted(set(Y_MEMBERS[0] + Y_MEMBERS[1] + Z_MEMBERS[0] + Z_MEMBERS[1])):
                values[m] = state[0, SLOT[m], x + 1, rows_of(group), :]
            pack(0, x, group, values)
        return carry

    lax.fori_loop(0, NX, first_pack, 0)
    state[0, 0, 1, pl.ds(ROW0, NY), :] = state[0, SLOT[9], 1, pl.ds(ROW0, NY), :]
    loads[20].wait()
    loads[21].wait()

    def message(b, m):
        cells = pl.ds(ROW0, NY)
        if m == 1:
            return state.at[b, pl.ds(0, 5), 1, cells, :], state.at[b, pl.ds(0, 5), NX + 1, cells, :]
        if m == 2:
            return state.at[b, pl.ds(8, 5), NX, cells, :], state.at[b, pl.ds(8, 5), 0, cells, :]
        if m in (3, 4):
            return ysend.at[b, m - 3], yrecv.at[b, m - 3]
        if m in (5, 6):
            return zsend.at[b, m - 5], zrecv.at[b, m - 5, cells, :]
        vector = LATTICE[m]
        if m <= 10:
            side = 0 if vector[1] > 0 else 1
            start = 0 if vector[0] > 0 else NX - 8
            member = Y_MEMBERS[side].index(m)
            return ysend.at[b, side, member, pl.ds(start, 8), :], xyrecv.at[b, m - 7]
        side = 0 if vector[2] > 0 else 1
        if m <= 14:
            return zsend.at[b, side], xzrecv.at[b, m - 11]
        start = 0 if vector[1] > 0 else NY - 8
        return zsend.at[b, side, pl.ds(start, 8), :], yzrecv.at[b, m - 15]

    def copy_of(t, b, m, target):
        source, landing = message(b, m)
        return pltpu.make_async_remote_copy(
            src_ref=source,
            dst_ref=landing,
            send_sem=send_sem.at[t, m - 1],
            recv_sem=recv_sem.at[t, m - 1],
            device_id=target,
            device_id_type=MESH,
        )

    def exchange(t, b):
        for m in range(1, 19):
            at, inside = beside(LATTICE[m], -1)

            @pl.when(inside)
            def _():
                copy_of(t, b, m, at).start()

        for m in range(1, 19):
            at, inside = beside(LATTICE[m], 1)

            @pl.when(inside)
            def _():
                copy_of(t, b, m, at).wait_recv()

        for m in range(1, 19):
            at, inside = beside(LATTICE[m], -1)

            @pl.when(inside)
            def _():
                copy_of(t, b, m, at).wait_send()

    def unpack(b):
        state[b, SLOT[9], NX + 1, pl.ds(ROW0, NY), :] = state[b, 0, NX + 1, pl.ds(ROW0, NY), :]
        for side in range(2):
            row = ROW0 + NY if side == 0 else ROW0 - 1
            for i, m in enumerate(Y_MEMBERS[side]):
                for x in range(NX):
                    state[b, SLOT[m], x + 1, pl.ds(row, 1), :] = yrecv[b, side, i, pl.ds(x, 1), :]
        for m in range(7, 11):
            vector = LATTICE[m]
            plane = NX + 1 if vector[0] > 0 else 0
            row = ROW0 + NY if vector[1] > 0 else ROW0 - 1
            source = 0 if vector[0] > 0 else 7
            state[b, SLOT[m], plane, pl.ds(row, 1), :] = xyrecv[b, m - 7, pl.ds(source, 1), :]
        for m in range(11, 15):
            vector = LATTICE[m]
            side = 0 if vector[2] > 0 else 1
            i = Z_MEMBERS[side].index(m)
            source = i * LANES + (1 if vector[0] > 0 else NX)
            place = i * LANES + (NX + 1 if vector[0] > 0 else 0)
            for group in range(GROUPS):
                moved = pltpu.roll(
                    xzrecv[b, m - 11, pl.ds(8 * group, 8), :], (place - source) % NZ, 1
                )
                zrecv[b, side, rows_of(group), :] = jnp.where(
                    lane == place, moved, zrecv[b, side, rows_of(group), :]
                )
        for m in range(15, 19):
            vector = LATTICE[m]
            side = 0 if vector[2] > 0 else 1
            row = ROW0 + NY if vector[1] > 0 else ROW0 - 1
            source = 0 if vector[1] > 0 else 7
            zrecv[b, side, pl.ds(row, 1), :] = yzrecv[b, m - 15, pl.ds(source, 1), :]

    def pull(b, x, group):
        read = []
        for m in range(19):
            vector = LATTICE[m]
            value = state[b, SLOT[m], x + 1 + vector[0], rows_of(group, vector[1]), :]
            if vector[2] != 0:
                side = 0 if vector[2] > 0 else 1
                place = Z_MEMBERS[side].index(m) * LANES + x + 1 + vector[0]
                column = zrecv[b, side, rows_of(group, vector[1]), :]
                if side == 0:
                    value = jnp.where(
                        lane == NZ - 1,
                        pltpu.roll(column, NZ - 1 - place, 1),
                        pltpu.roll(value, NZ - 1, 1),
                    )
                else:
                    value = jnp.where(
                        lane == 0,
                        pltpu.roll(column, NZ - place, 1),
                        pltpu.roll(value, 1, 1),
                    )
            read.append(value)
        return read

    def collide(read, u, is_solid):
        face_sum = [read[1] + read[2], read[3] + read[4], read[5] + read[6]]
        face_dif = [read[1] - read[2], read[3] - read[4], read[5] - read[6]]
        sums, twist, first, second = [], [], [], []
        for m in (7, 11, 15):
            plus, minus = read[m] + read[m + 1], read[m + 2] + read[m + 3]
            dplus, dminus = read[m] - read[m + 1], read[m + 2] - read[m + 3]
            sums.append(plus + minus)
            twist.append(plus - minus)
            first.append(dplus + dminus)
            second.append(dplus - dminus)
        xy, xz, yz = 0, 1, 2
        twice = [value + value for value in face_sum]
        rho = 12.0 * read[0] + (twice[0] + twice[1] + twice[2]) + (sums[xy] + sums[xz] + sums[yz])
        edge = [first[xy] + first[xz], second[xy] + first[yz], second[xz] + second[yz]]
        flux = [(face_dif[k] + face_dif[k]) + edge[k] for k in range(3)]
        stress = [
            twice[0] + (sums[xy] + sums[xz]),
            twice[1] + (sums[xy] + sums[yz]),
            twice[2] + (sums[xz] + sums[yz]),
        ]
        u3 = [3.0 * value for value in u]
        w = [
            rho * u[0] - (stress[0] * u3[0] + twist[xy] * u3[1] + twist[xz] * u3[2]),
            rho * u[1] - (twist[xy] * u3[0] + stress[1] * u3[1] + twist[yz] * u3[2]),
            rho * u[2] - (twist[xz] * u3[0] + twist[yz] * u3[1] + stress[2] * u3[2]),
        ]
        g = [(OMEGA * 3.0 / 36.0) * (flux[k] - w[k]) for k in range(3)]
        base = (OMEGA / 36.0) * rho + (OMEGA * 1.5 / 36.0) * (u[0] * w[0] + u[1] * w[1] + u[2] * w[2])
        along = [None] * 19
        along[0] = base
        for k in range(3):
            along[1 + 2 * k] = base + g[k]
            along[2 + 2 * k] = base - g[k]
        for m, (j, k) in ((7, (0, 1)), (11, (0, 2)), (15, (1, 2))):
            total, difference = g[j] + g[k], g[j] - g[k]
            along[m], along[m + 1] = base + total, base - total
            along[m + 2], along[m + 3] = base + difference, base - difference
        outputs = [
            jnp.where(is_solid, read[OPPOSITE[m]], along[m] + (1.0 - OMEGA) * read[m])
            for m in range(19)
        ]
        momentum = face_dif[2] + edge[2]
        pressure = jnp.where(is_solid, -momentum, 10.0 * g[2] + (1.0 - OMEGA) * momentum)
        return outputs, pressure

    out_row = lax.broadcasted_iota(jnp.int32, (128, NZ), 0)
    out_lane = lax.broadcasted_iota(jnp.int32, (128, NZ), 1)
    same_y = (out_row & 7) == (out_lane >> 4)
    own_lane = lax.broadcasted_iota(jnp.int32, (8, NZ), 0) == (lane >> 4)

    def one_step(t):
        b = t % 2
        nb = 1 - b
        exchange(t, b)
        unpack(b)
        acc[...] = jnp.zeros_like(acc)

        def one_plane(x, inner):
            for group in range(GROUPS):
                rows = pl.ds(8 * group, 8)
                read = pull(b, x, group)
                u = [vel[STEPS - 1 - t, k, x, rows, :] for k in range(3)]
                outputs, pressure = collide(read, u, solid[x, rows, :] == 1)
                for m in range(19):
                    state[nb, SLOT[m], x + 1, rows_of(group), :] = outputs[m]
                pack(nb, x, group, outputs)
                upper = pressure.astype(jnp.bfloat16).astype(jnp.float32)
                both = jnp.concatenate([upper, pressure - upper], axis=0).astype(jnp.bfloat16)
                high = (ids[x, rows, :] >> 4).astype(jnp.float32)
                high = jnp.concatenate([high, high], axis=0).astype(jnp.bfloat16)
                for h in range(8):
                    hi_part[pl.ds(16 * h, 16), pl.ds(NZ * group, NZ)] = jnp.where(
                        high == h, both, jnp.zeros_like(both)
                    )
            acc[...] += lax.dot_general(
                hi_part[...],
                lo_hot[x],
                (((1,), (1,)), ((), ())),
                preferred_element_type=jnp.float32,
            )
            return inner

        lax.fori_loop(0, NX, one_plane, 0)
        state[nb, 0, 1, pl.ds(ROW0, NY), :] = state[nb, SLOT[9], 1, pl.ds(ROW0, NY), :]

        own = jnp.where(same_y, acc[...], 0.0)
        total = jnp.sum(own.reshape(8, 16, NZ), axis=1)
        for shift in (64, 32, 16):
            total = total + pltpu.roll(total, shift, 1)
        sums[pl.ds(STEPS - 1 - t, 1), :] = jnp.sum(
            jnp.where(own_lane, total, 0.0), axis=0, keepdims=True
        )

    for t in range(STEPS):
        one_step(t)

    def gather_sum(own, slots, place, others, sems):
        slots[place] = own
        copies = []
        for k, target in enumerate(others):
            copies.append(
                pltpu.make_async_remote_copy(
                    src_ref=slots.at[place],
                    dst_ref=slots.at[place],
                    send_sem=sems.at[0, k],
                    recv_sem=sems.at[1, k],
                    device_id=target,
                    device_id_type=MESH,
                )
            )
        for copy in copies:
            copy.start()
        for copy in copies:
            copy.wait()
        total = slots[0]
        for k in range(1, len(others) + 1):
            total = total + slots[k]
        return total

    stores = []
    for m in range(19):
        stores.append(
            pltpu.make_async_copy(
                state.at[STEPS % 2, SLOT[m], pl.ds(1, NX), pl.ds(ROW0, NY), :],
                out_ref.at[m],
                out_sem.at[m],
            )
        )
    for store in stores:
        store.start()
    sums[pl.ds(STEPS, 8 - STEPS), :] = jnp.zeros((8 - STEPS, NZ), jnp.float32)
    total = gather_sum(sums[...], wall_xy, me[0] * sizes[1] + me[1], xy_others, xy_sem)
    total = gather_sum(total, wall_z, me[2], z_others, z_sem)
    cells_all = NX * NY * NZ * sizes[0] * sizes[1] * sizes[2]
    wall_ref[...] = total[:STEPS] * ((cells_all / (2.0 * WALLS)) ** (-0.5))
    for store in stores:
        store.wait()


def body(terminal_adjoint, saved_velocity, solid_mask, wall_ids):
    sizes = tuple(lax.axis_size(name) for name in ("gx", "gy", "gz"))
    f32, vmem = jnp.float32, pltpu.VMEM
    return pl.pallas_call(
        functools.partial(kernel, sizes),
        out_shape=(
            jax.ShapeDtypeStruct((19, NX, NY, NZ), f32),
            jax.ShapeDtypeStruct((STEPS, WALLS), f32),
        ),
        in_specs=[pl.BlockSpec(memory_space=pltpu.HBM)] * 4,
        out_specs=(pl.BlockSpec(memory_space=pl.ANY), pl.BlockSpec(memory_space=pltpu.VMEM)),
        scratch_shapes=[
            vmem((2, SLOTS, NX + 2, ROWS, NZ), f32),
            vmem((STEPS, 3, NX, NY, NZ), f32),
            vmem((NX, NY, NZ), jnp.int32),
            vmem((NX, NY, NZ), jnp.int32),
            vmem((2, 2, 5, NX, NZ), f32),
            vmem((2, 2, 5, NX, NZ), f32),
            vmem((2, 2, NY, NZ), f32),
            vmem((2, 2, ROWS, NZ), f32),
            vmem((2, 4, 8, NZ), f32),
            vmem((2, 4, NY, NZ), f32),
            vmem((2, 4, 8, NZ), f32),
            vmem((NX, 128, GROUPS * NZ), jnp.bfloat16),
            vmem((128, GROUPS * NZ), jnp.bfloat16),
            vmem((128, NZ), f32),
            vmem((8, NZ), f32),
            vmem((sizes[0] * sizes[1], 8, NZ), f32),
            vmem((sizes[2], 8, NZ), f32),
            pltpu.SemaphoreType.DMA((22,)),
            pltpu.SemaphoreType.DMA((19,)),
            pltpu.SemaphoreType.DMA((STEPS, 18)),
            pltpu.SemaphoreType.DMA((STEPS, 18)),
            pltpu.SemaphoreType.DMA((2, max(1, sizes[0] * sizes[1] - 1))),
            pltpu.SemaphoreType.DMA((2, max(1, sizes[2] - 1))),
        ],
        compiler_params=pltpu.CompilerParams(
            collective_id=0, has_side_effects=True, vmem_limit_bytes=48 * 2**20
        ),
        name="adjoint_steps",
    )(terminal_adjoint, saved_velocity, solid_mask, wall_ids)


def solution(mesh):
    return jax.shard_map(
        body,
        mesh=mesh,
        in_specs=(
            P(None, "gx", "gy", "gz"),
            P(None, None, "gx", "gy", "gz"),
            P("gx", "gy", "gz"),
            P("gx", "gy", "gz"),
        ),
        out_specs=(P(None, "gx", "gy", "gz"), P()),
        check_vma=False,
    )
```

```python
import functools

import jax
import jax.numpy as jnp
from jax import lax
from jax.experimental import pallas as pl
from jax.experimental.pallas import tpu as pltpu
from jax.sharding import PartitionSpec as P

STEPS = 4
WALLS = 128
OMEGA = 1.25
LATTICE = (
    (0, 0, 0),
    (1, 0, 0),
    (-1, 0, 0),
    (0, 1, 0),
    (0, -1, 0),
    (0, 0, 1),
    (0, 0, -1),
    (1, 1, 0),
    (-1, -1, 0),
    (1, -1, 0),
    (-1, 1, 0),
    (1, 0, 1),
    (-1, 0, -1),
    (1, 0, -1),
    (-1, 0, 1),
    (0, 1, 1),
    (0, -1, -1),
    (0, 1, -1),
    (0, -1, 1),
)
OPPOSITE = (0, 2, 1, 4, 3, 6, 5, 8, 7, 10, 9, 12, 11, 14, 13, 16, 15, 18, 17)

NX, NY, NZ = 16, 32, 128
ROW0 = 8
ROWS = 48
GROUPS = NY // 8

SLOT = {9: 16, 1: 1, 11: 2, 13: 3, 7: 4, 3: 5, 15: 6, 17: 7, 10: 8, 2: 9,
        12: 10, 14: 11, 8: 12, 4: 13, 16: 14, 18: 15, 5: 17, 6: 18, 0: 19}
SLOTS = 20
Y_MEMBERS = ((7, 3, 15, 17, 10), (8, 4, 16, 18, 9))
Z_MEMBERS = ((5, 11, 14, 15, 18), (6, 12, 13, 16, 17))
LANES = NX + 2
MESH = pl.DeviceIdType.MESH


def kernel(
    sizes, adj_ref, vel_ref, solid_ref, ids_ref, out_ref, wall_ref,
    state0, state1, vel, solid, ids, ysend, yrecv, zsend, zrecv, xyrecv, xzrecv, yzrecv,
    lo_hot, hi_part, acc, sums, wall_xy, wall_z,
    in_sem, send_sem, recv_sem, xy_sem, z_sem,
):
    state = (state0, state1)
    me = (lax.axis_index("gx"), lax.axis_index("gy"), lax.axis_index("gz"))

    loads = []
    for m in range(19):
        loads.append(
            pltpu.make_async_copy(
                adj_ref.at[m],
                state[0].at[SLOT[m], pl.ds(1, NX), pl.ds(ROW0, NY), :],
                in_sem.at[m],
            )
        )
    loads.append(pltpu.make_async_copy(ids_ref, ids, in_sem.at[19]))
    loads.append(pltpu.make_async_copy(solid_ref, solid, in_sem.at[20]))
    loads.append(pltpu.make_async_copy(vel_ref, vel, in_sem.at[21]))
    for load in loads:
        load.start()

    zero_plane = jnp.zeros((SLOTS, ROWS, NZ), jnp.float32)
    for b in range(2):
        state[b][:, 0] = zero_plane
        state[b][:, NX + 1] = zero_plane
    yrecv[...] = jnp.zeros_like(yrecv)
    zrecv[...] = jnp.zeros_like(zrecv)
    xyrecv[...] = jnp.zeros_like(xyrecv)
    xzrecv[...] = jnp.zeros_like(xzrecv)
    yzrecv[...] = jnp.zeros_like(yzrecv)

    def beside(vector, sign):
        at = tuple(me[k] + sign * vector[k] for k in range(3))
        inside = None
        for k in range(3):
            if vector[k] != 0:
                here = (at[k] >= 0) & (at[k] < sizes[k])
                inside = here if inside is None else inside & here
        return at, inside

    barrier = pltpu.get_barrier_semaphore()
    count = jnp.int32(0)
    for m in range(1, 19):
        at, inside = beside(LATTICE[m], 1)
        count = count + inside.astype(jnp.int32)

        @pl.when(inside)
        def _():
            pl.semaphore_signal(barrier, inc=1, device_id=at, device_id_type=MESH)

    plane = sizes[0] * sizes[1]
    xy_others, z_others = [], []
    for k in range(1, plane):
        there = lax.rem(me[0] * sizes[1] + me[1] + k, plane)
        xy_others.append((there // sizes[1], lax.rem(there, sizes[1]), me[2]))
    for k in range(1, sizes[2]):
        z_others.append((me[0], me[1], lax.rem(me[2] + k, sizes[2])))
    for target in xy_others + z_others:
        pl.semaphore_signal(barrier, inc=1, device_id=target, device_id_type=MESH)

    lane = lax.broadcasted_iota(jnp.int32, (8, NZ), 1)

    def rows_of(group, shift=0):
        return pl.ds(ROW0 + 8 * group + shift, 8)

    loads[19].wait()
    low_iota = lax.broadcasted_iota(jnp.int32, (16, NZ), 0)

    def hot_plane(x, carry):
        for group in range(GROUPS):
            low = ids[x, pl.ds(8 * group, 8), :] & 15
            for y in range(8):
                hot = jnp.broadcast_to(low[y : y + 1, :], (16, NZ)) == low_iota
                lo_hot[x, pl.ds(16 * y, 16), pl.ds(NZ * group, NZ)] = jnp.where(
                    hot, 1.0, 0.0
                ).astype(jnp.bfloat16)
        return carry

    lax.fori_loop(0, NX, hot_plane, 0)

    def pack(b, x, group, values):
        for side in range(2):
            rows = pl.ds(8 * group, 8)
            packed = zsend[b, side, rows, :]
            for i, m in enumerate(Z_MEMBERS[side]):
                place = i * LANES + x + 1
                moved = pltpu.roll(values[m], place + side, 1)
                packed = jnp.where(lane == place, moved, packed)
            zsend[b, side, rows, :] = packed
        if group == 0:
            for i, m in enumerate(Y_MEMBERS[0]):
                ysend[b, 0, i, pl.ds(x, 1), :] = values[m][0:1, :]
        if group == GROUPS - 1:
            for i, m in enumerate(Y_MEMBERS[1]):
                ysend[b, 1, i, pl.ds(x, 1), :] = values[m][7:8, :]

    for m in range(19):
        loads[m].wait()

    def first_pack(x, carry):
        for group in range(GROUPS):
            values = {}
            for m in sorted(set(Y_MEMBERS[0] + Y_MEMBERS[1] + Z_MEMBERS[0] + Z_MEMBERS[1])):
                values[m] = state[0][SLOT[m], x + 1, rows_of(group), :]
            pack(0, x, group, values)
        return carry

    lax.fori_loop(0, NX, first_pack, 0)
    state[0][0, 1, pl.ds(ROW0, NY), :] = state[0][SLOT[9], 1, pl.ds(ROW0, NY), :]
    pl.semaphore_wait(barrier, count + len(xy_others) + len(z_others))
    loads[20].wait()
    loads[21].wait()

    def message(b, m):
        cells = pl.ds(ROW0, NY)
        if m == 1:
            return state[b].at[pl.ds(0, 5), 1, cells, :], state[b].at[pl.ds(0, 5), NX + 1, cells, :]
        if m == 2:
            return state[b].at[pl.ds(8, 5), NX, cells, :], state[b].at[pl.ds(8, 5), 0, cells, :]
        if m in (3, 4):
            return ysend.at[b, m - 3], yrecv.at[b, m - 3]
        if m in (5, 6):
            return zsend.at[b, m - 5], zrecv.at[b, m - 5, cells, :]
        vector = LATTICE[m]
        if m <= 10:
            side = 0 if vector[1] > 0 else 1
            start = 0 if vector[0] > 0 else NX - 8
            member = Y_MEMBERS[side].index(m)
            return ysend.at[b, side, member, pl.ds(start, 8), :], xyrecv.at[b, m - 7]
        side = 0 if vector[2] > 0 else 1
        if m <= 14:
            return zsend.at[b, side], xzrecv.at[b, m - 11]
        start = 0 if vector[1] > 0 else NY - 8
        return zsend.at[b, side, pl.ds(start, 8), :], yzrecv.at[b, m - 15]

    def copy_of(t, b, m, target):
        source, landing = message(b, m)
        return pltpu.make_async_remote_copy(
            src_ref=source,
            dst_ref=landing,
            send_sem=send_sem.at[t, m - 1],
            recv_sem=recv_sem.at[t, m - 1],
            device_id=target,
            device_id_type=MESH,
        )

    def exchange(t, b):
        for m in range(1, 19):
            at, inside = beside(LATTICE[m], -1)

            @pl.when(inside)
            def _():
                copy_of(t, b, m, at).start()

        for m in range(1, 19):
            at, inside = beside(LATTICE[m], 1)

            @pl.when(inside)
            def _():
                copy_of(t, b, m, at).wait_recv()

    def sent(t, b):
        for m in range(1, 19):
            at, inside = beside(LATTICE[m], -1)

            @pl.when(inside)
            def _():
                copy_of(t, b, m, at).wait_send()

    def unpack(b):
        state[b][SLOT[9], NX + 1, pl.ds(ROW0, NY), :] = state[b][0, NX + 1, pl.ds(ROW0, NY), :]
        for side in range(2):
            row = ROW0 + NY if side == 0 else ROW0 - 1
            for i, m in enumerate(Y_MEMBERS[side]):
                for x in range(NX):
                    state[b][SLOT[m], x + 1, pl.ds(row, 1), :] = yrecv[b, side, i, pl.ds(x, 1), :]
        for m in range(7, 11):
            vector = LATTICE[m]
            plane = NX + 1 if vector[0] > 0 else 0
            row = ROW0 + NY if vector[1] > 0 else ROW0 - 1
            source = 0 if vector[0] > 0 else 7
            state[b][SLOT[m], plane, pl.ds(row, 1), :] = xyrecv[b, m - 7, pl.ds(source, 1), :]
        for m in range(11, 15):
            vector = LATTICE[m]
            side = 0 if vector[2] > 0 else 1
            i = Z_MEMBERS[side].index(m)
            source = i * LANES + (1 if vector[0] > 0 else NX)
            place = i * LANES + (NX + 1 if vector[0] > 0 else 0)
            for group in range(GROUPS):
                moved = pltpu.roll(
                    xzrecv[b, m - 11, pl.ds(8 * group, 8), :], (place - source) % NZ, 1
                )
                zrecv[b, side, rows_of(group), :] = jnp.where(
                    lane == place, moved, zrecv[b, side, rows_of(group), :]
                )
        for m in range(15, 19):
            vector = LATTICE[m]
            side = 0 if vector[2] > 0 else 1
            row = ROW0 + NY if vector[1] > 0 else ROW0 - 1
            source = 0 if vector[1] > 0 else 7
            zrecv[b, side, pl.ds(row, 1), :] = yzrecv[b, m - 15, pl.ds(source, 1), :]

    def pull(b, x, group):
        read = []
        for m in range(19):
            vector = LATTICE[m]
            value = state[b][SLOT[m], x + 1 + vector[0], rows_of(group, vector[1]), :]
            if vector[2] != 0:
                side = 0 if vector[2] > 0 else 1
                place = Z_MEMBERS[side].index(m) * LANES + x + 1 + vector[0]
                column = zrecv[b, side, rows_of(group, vector[1]), :]
                if side == 0:
                    value = jnp.where(
                        lane == NZ - 1,
                        pltpu.roll(column, NZ - 1 - place, 1),
                        pltpu.roll(value, NZ - 1, 1),
                    )
                else:
                    value = jnp.where(
                        lane == 0,
                        pltpu.roll(column, NZ - place, 1),
                        pltpu.roll(value, 1, 1),
                    )
            read.append(value)
        return read

    def collide(read, u, is_solid):
        face_sum = [read[1] + read[2], read[3] + read[4], read[5] + read[6]]
        face_dif = [read[1] - read[2], read[3] - read[4], read[5] - read[6]]
        sums, twist, first, second = [], [], [], []
        for m in (7, 11, 15):
            plus, minus = read[m] + read[m + 1], read[m + 2] + read[m + 3]
            dplus, dminus = read[m] - read[m + 1], read[m + 2] - read[m + 3]
            sums.append(plus + minus)
            twist.append(plus - minus)
            first.append(dplus + dminus)
            second.append(dplus - dminus)
        xy, xz, yz = 0, 1, 2
        twice = [value + value for value in face_sum]
        rho = 12.0 * read[0] + (twice[0] + twice[1] + twice[2]) + (sums[xy] + sums[xz] + sums[yz])
        edge = [first[xy] + first[xz], second[xy] + first[yz], second[xz] + second[yz]]
        flux = [(face_dif[k] + face_dif[k]) + edge[k] for k in range(3)]
        stress = [
            twice[0] + (sums[xy] + sums[xz]),
            twice[1] + (sums[xy] + sums[yz]),
            twice[2] + (sums[xz] + sums[yz]),
        ]
        u3 = [3.0 * value for value in u]
        w = [
            rho * u[0] - (stress[0] * u3[0] + twist[xy] * u3[1] + twist[xz] * u3[2]),
            rho * u[1] - (twist[xy] * u3[0] + stress[1] * u3[1] + twist[yz] * u3[2]),
            rho * u[2] - (twist[xz] * u3[0] + twist[yz] * u3[1] + stress[2] * u3[2]),
        ]
        g = [(OMEGA * 3.0 / 36.0) * (flux[k] - w[k]) for k in range(3)]
        base = (OMEGA / 36.0) * rho + (OMEGA * 1.5 / 36.0) * (u[0] * w[0] + u[1] * w[1] + u[2] * w[2])
        along = [None] * 19
        along[0] = base
        for k in range(3):
            along[1 + 2 * k] = base + g[k]
            along[2 + 2 * k] = base - g[k]
        for m, (j, k) in ((7, (0, 1)), (11, (0, 2)), (15, (1, 2))):
            total, difference = g[j] + g[k], g[j] - g[k]
            along[m], along[m + 1] = base + total, base - total
            along[m + 2], along[m + 3] = base + difference, base - difference
        outputs = [
            jnp.where(is_solid, read[OPPOSITE[m]], along[m] + (1.0 - OMEGA) * read[m])
            for m in range(19)
        ]
        momentum = face_dif[2] + edge[2]
        pressure = jnp.where(is_solid, -momentum, 10.0 * g[2] + (1.0 - OMEGA) * momentum)
        return outputs, pressure

    out_row = lax.broadcasted_iota(jnp.int32, (128, NZ), 0)
    out_lane = lax.broadcasted_iota(jnp.int32, (128, NZ), 1)
    same_y = (out_row & 7) == (out_lane >> 4)
    own_lane = lax.broadcasted_iota(jnp.int32, (8, NZ), 0) == (lane >> 4)

    def one_step(t):
        b = t % 2
        nb = 1 - b
        exchange(t, b)
        unpack(b)
        acc[...] = jnp.zeros_like(acc)

        def one_plane(x, inner):
            for group in range(GROUPS):
                rows = pl.ds(8 * group, 8)
                read = pull(b, x, group)
                u = [vel[STEPS - 1 - t, k, x, rows, :] for k in range(3)]
                outputs, pressure = collide(read, u, solid[x, rows, :] == 1)
                for m in range(19):
                    if t < STEPS - 1:
                        state[nb][SLOT[m], x + 1, rows_of(group), :] = outputs[m]
                    else:
                        out_ref[m, x, rows, :] = outputs[m]
                if t < STEPS - 1:
                    pack(nb, x, group, outputs)
                upper = pressure.astype(jnp.bfloat16).astype(jnp.float32)
                both = jnp.concatenate([upper, pressure - upper], axis=0).astype(jnp.bfloat16)
                high = (ids[x, rows, :] >> 4).astype(jnp.float32)
                high = jnp.concatenate([high, high], axis=0).astype(jnp.bfloat16)
                for h in range(8):
                    hi_part[pl.ds(16 * h, 16), pl.ds(NZ * group, NZ)] = jnp.where(
                        high == h, both, jnp.zeros_like(both)
                    )
            acc[...] += lax.dot_general(
                hi_part[...],
                lo_hot[x],
                (((1,), (1,)), ((), ())),
                preferred_element_type=jnp.float32,
            )
            return inner

        def two_planes(pair, inner):
            one_plane(2 * pair, inner)
            return one_plane(2 * pair + 1, inner)

        lax.fori_loop(0, NX // 2, two_planes, 0)
        sent(t, b)
        if t < STEPS - 1:
            state[nb][0, 1, pl.ds(ROW0, NY), :] = state[nb][SLOT[9], 1, pl.ds(ROW0, NY), :]

        own = jnp.where(same_y, acc[...], 0.0)
        total = jnp.sum(own.reshape(8, 16, NZ), axis=1)
        for shift in (64, 32, 16):
            total = total + pltpu.roll(total, shift, 1)
        sums[pl.ds(STEPS - 1 - t, 1), :] = jnp.sum(
            jnp.where(own_lane, total, 0.0), axis=0, keepdims=True
        )

    for t in range(STEPS):
        one_step(t)

    def gather_sum(own, slots, place, others, sems):
        slots[place] = own
        copies = []
        for k, target in enumerate(others):
            copies.append(
                pltpu.make_async_remote_copy(
                    src_ref=slots.at[place],
                    dst_ref=slots.at[place],
                    send_sem=sems.at[0, k],
                    recv_sem=sems.at[1, k],
                    device_id=target,
                    device_id_type=MESH,
                )
            )
        for copy in copies:
            copy.start()
        for copy in copies:
            copy.wait()
        total = slots[0]
        for k in range(1, len(others) + 1):
            total = total + slots[k]
        return total

    sums[pl.ds(STEPS, 8 - STEPS), :] = jnp.zeros((8 - STEPS, NZ), jnp.float32)
    total = gather_sum(sums[...], wall_xy, me[0] * sizes[1] + me[1], xy_others, xy_sem)
    total = gather_sum(total, wall_z, me[2], z_others, z_sem)
    cells_all = NX * NY * NZ * sizes[0] * sizes[1] * sizes[2]
    wall_ref[...] = total[:STEPS] * ((cells_all / (2.0 * WALLS)) ** (-0.5))


def body(terminal_adjoint, saved_velocity, solid_mask, wall_ids):
    sizes = tuple(lax.axis_size(name) for name in ("gx", "gy", "gz"))
    f32, vmem = jnp.float32, pltpu.VMEM
    return pl.pallas_call(
        functools.partial(kernel, sizes),
        out_shape=(
            pltpu.VMEM((19, NX, NY, NZ), f32),
            jax.ShapeDtypeStruct((STEPS, WALLS), f32),
        ),
        in_specs=[pl.BlockSpec(memory_space=pltpu.HBM)] * 4,
        out_specs=(pl.BlockSpec(memory_space=pltpu.VMEM),) * 2,
        scratch_shapes=[
            vmem((SLOTS, NX + 2, ROWS, NZ), f32),
            vmem((SLOTS, NX + 2, ROWS, NZ), f32),
            vmem((STEPS, 3, NX, NY, NZ), f32),
            vmem((NX, NY, NZ), jnp.int32),
            vmem((NX, NY, NZ), jnp.int32),
            vmem((2, 2, 5, NX, NZ), f32),
            vmem((2, 2, 5, NX, NZ), f32),
            vmem((2, 2, NY, NZ), f32),
            vmem((2, 2, ROWS, NZ), f32),
            vmem((2, 4, 8, NZ), f32),
            vmem((2, 4, NY, NZ), f32),
            vmem((2, 4, 8, NZ), f32),
            vmem((NX, 128, GROUPS * NZ), jnp.bfloat16),
            vmem((128, GROUPS * NZ), jnp.bfloat16),
            vmem((128, NZ), f32),
            vmem((8, NZ), f32),
            vmem((sizes[0] * sizes[1], 8, NZ), f32),
            vmem((sizes[2], 8, NZ), f32),
            pltpu.SemaphoreType.DMA((22,)),
            pltpu.SemaphoreType.DMA((STEPS, 18)),
            pltpu.SemaphoreType.DMA((STEPS, 18)),
            pltpu.SemaphoreType.DMA((2, max(1, sizes[0] * sizes[1] - 1))),
            pltpu.SemaphoreType.DMA((2, max(1, sizes[2] - 1))),
        ],
        compiler_params=pltpu.CompilerParams(
            collective_id=0, has_side_effects=True, vmem_limit_bytes=58 * 2**20
        ),
        name="adjoint_steps",
    )(terminal_adjoint, saved_velocity, solid_mask, wall_ids)


def solution(mesh):
    return jax.shard_map(
        body,
        mesh=mesh,
        in_specs=(
            P(None, "gx", "gy", "gz"),
            P(None, None, "gx", "gy", "gz"),
            P("gx", "gy", "gz"),
            P("gx", "gy", "gz"),
        ),
        out_specs=(P(None, "gx", "gy", "gz"), P()),
        check_vma=False,
    )
```

```python
import functools

import jax
import jax.numpy as jnp
from jax import lax
from jax.experimental import pallas as pl
from jax.experimental.pallas import tpu as pltpu
from jax.sharding import PartitionSpec as P

STEPS = 4
WALLS = 128
OMEGA = 1.25
LATTICE = (
    (0, 0, 0),
    (1, 0, 0),
    (-1, 0, 0),
    (0, 1, 0),
    (0, -1, 0),
    (0, 0, 1),
    (0, 0, -1),
    (1, 1, 0),
    (-1, -1, 0),
    (1, -1, 0),
    (-1, 1, 0),
    (1, 0, 1),
    (-1, 0, -1),
    (1, 0, -1),
    (-1, 0, 1),
    (0, 1, 1),
    (0, -1, -1),
    (0, 1, -1),
    (0, -1, 1),
)
OPPOSITE = (0, 2, 1, 4, 3, 6, 5, 8, 7, 10, 9, 12, 11, 14, 13, 16, 15, 18, 17)

NX, NY, NZ = 16, 32, 128
ROW0 = 8
ROWS = 48
GROUPS = NY // 8

SLOT = {9: 16, 1: 1, 11: 2, 13: 3, 7: 4, 3: 5, 15: 6, 17: 7, 10: 8, 2: 9,
        12: 10, 14: 11, 8: 12, 4: 13, 16: 14, 18: 15, 5: 17, 6: 18, 0: 19}
SLOTS = 20
Y_MEMBERS = ((7, 3, 15, 17, 10), (8, 4, 16, 18, 9))
Z_MEMBERS = ((5, 11, 14, 15, 18), (6, 12, 13, 16, 17))
LANES = NX + 2
PAIRS = NX // 2
QUARTER = PAIRS // 2
INNER_MESSAGES = (3, 4, 5, 6, 15, 16, 17, 18)
MESH = pl.DeviceIdType.MESH


def kernel(
    sizes, adj_ref, vel_ref, solid_ref, ids_ref, out_ref, wall_ref,
    state0, state1, vel, solid, ids, ysend, yrecv, zsend, zrecv, zinner, xyrecv, xzrecv, yzrecv,
    lo_hot, hi_part, acc, sums, wall_xy, wall_z,
    in_sem, send_sem, recv_sem, xy_sem, z_sem,
):
    state = (state0, state1)
    me = (lax.axis_index("gx"), lax.axis_index("gy"), lax.axis_index("gz"))

    loads = []
    for m in range(19):
        loads.append(
            pltpu.make_async_copy(
                adj_ref.at[m],
                state[0].at[SLOT[m], pl.ds(1, NX), pl.ds(ROW0, NY), :],
                in_sem.at[m],
            )
        )
    loads.append(pltpu.make_async_copy(ids_ref, ids, in_sem.at[19]))
    loads.append(pltpu.make_async_copy(solid_ref, solid, in_sem.at[20]))
    loads.append(pltpu.make_async_copy(vel_ref, vel, in_sem.at[21]))
    for load in loads:
        load.start()

    zero_plane = jnp.zeros((SLOTS, ROWS, NZ), jnp.float32)
    for b in range(2):
        state[b][:, 0] = zero_plane
        state[b][:, NX + 1] = zero_plane
    yrecv[...] = jnp.zeros_like(yrecv)
    zrecv[...] = jnp.zeros_like(zrecv)
    zinner[...] = jnp.zeros_like(zinner)
    xyrecv[...] = jnp.zeros_like(xyrecv)
    xzrecv[...] = jnp.zeros_like(xzrecv)
    yzrecv[...] = jnp.zeros_like(yzrecv)

    def beside(vector, sign):
        at = tuple(me[k] + sign * vector[k] for k in range(3))
        inside = None
        for k in range(3):
            if vector[k] != 0:
                here = (at[k] >= 0) & (at[k] < sizes[k])
                inside = here if inside is None else inside & here
        return at, inside

    barrier = pltpu.get_barrier_semaphore()
    count = jnp.int32(0)
    for m in range(1, 19):
        at, inside = beside(LATTICE[m], 1)
        count = count + inside.astype(jnp.int32)

        @pl.when(inside)
        def _():
            pl.semaphore_signal(barrier, inc=1, device_id=at, device_id_type=MESH)

    plane = sizes[0] * sizes[1]
    xy_others, z_others = [], []
    for k in range(1, plane):
        there = lax.rem(me[0] * sizes[1] + me[1] + k, plane)
        xy_others.append((there // sizes[1], lax.rem(there, sizes[1]), me[2]))
    for k in range(1, sizes[2]):
        z_others.append((me[0], me[1], lax.rem(me[2] + k, sizes[2])))
    for target in xy_others + z_others:
        pl.semaphore_signal(barrier, inc=1, device_id=target, device_id_type=MESH)

    lane = lax.broadcasted_iota(jnp.int32, (8, NZ), 1)

    def rows_of(group, shift=0):
        return pl.ds(ROW0 + 8 * group + shift, 8)

    loads[19].wait()
    low_iota = lax.broadcasted_iota(jnp.int32, (16, NZ), 0)

    def hot_plane(x, carry):
        for group in range(GROUPS):
            low = ids[x, pl.ds(8 * group, 8), :] & 15
            for y in range(8):
                hot = jnp.broadcast_to(low[y : y + 1, :], (16, NZ)) == low_iota
                lo_hot[x, pl.ds(16 * y, 16), pl.ds(NZ * group, NZ)] = jnp.where(
                    hot, 1.0, 0.0
                ).astype(jnp.bfloat16)
        return carry

    lax.fori_loop(0, NX, hot_plane, 0)

    def pack(b, pair, high, group, values):
        part = pair // QUARTER
        x = NX - 1 - pair if high else pair
        row = lax.rem(pair, QUARTER)
        row = 2 * QUARTER - 1 - row if high else row
        for side in range(2):
            rows = pl.ds(8 * group, 8)
            packed = zsend[b, part, side, rows, :]
            for i, m in enumerate(Z_MEMBERS[side]):
                place = i * LANES + x + 1
                moved = pltpu.roll(values[m], place + side, 1)
                packed = jnp.where(lane == place, moved, packed)
            zsend[b, part, side, rows, :] = packed
        if group == 0:
            for i, m in enumerate(Y_MEMBERS[0]):
                ysend[b, part, 0, i, pl.ds(row, 1), :] = values[m][0:1, :]
        if group == GROUPS - 1:
            for i, m in enumerate(Y_MEMBERS[1]):
                ysend[b, part, 1, i, pl.ds(row, 1), :] = values[m][7:8, :]

    for m in range(19):
        loads[m].wait()

    def first_pack(pair, carry):
        for high in range(2):
            x = NX - 1 - pair if high else pair
            for group in range(GROUPS):
                values = {}
                for m in sorted(set(Y_MEMBERS[0] + Y_MEMBERS[1] + Z_MEMBERS[0] + Z_MEMBERS[1])):
                    values[m] = state[0][SLOT[m], x + 1, rows_of(group), :]
                pack(0, pair, high, group, values)
        return carry

    lax.fori_loop(0, PAIRS, first_pack, 0)
    state[0][0, 1, pl.ds(ROW0, NY), :] = state[0][SLOT[9], 1, pl.ds(ROW0, NY), :]
    pl.semaphore_wait(barrier, count + len(xy_others) + len(z_others))

    def message(b, part, m):
        cells = pl.ds(ROW0, NY)
        if m == 1:
            return state[b].at[pl.ds(0, 5), 1, cells, :], state[b].at[pl.ds(0, 5), NX + 1, cells, :]
        if m == 2:
            return state[b].at[pl.ds(8, 5), NX, cells, :], state[b].at[pl.ds(8, 5), 0, cells, :]
        if m in (3, 4):
            return ysend.at[b, part, m - 3], yrecv.at[b, part, m - 3]
        if m in (5, 6):
            landing = zinner if part else zrecv
            return zsend.at[b, part, m - 5], landing.at[b, m - 5, cells, :]
        vector = LATTICE[m]
        if m <= 10:
            side = 0 if vector[1] > 0 else 1
            return ysend.at[b, 0, side, Y_MEMBERS[side].index(m)], xyrecv.at[b, m - 7]
        side = 0 if vector[2] > 0 else 1
        if m <= 14:
            return zsend.at[b, 0, side], xzrecv.at[b, m - 11]
        start = 0 if vector[1] > 0 else NY - 8
        return zsend.at[b, part, side, pl.ds(start, 8), :], yzrecv.at[b, part, m - 15]

    def copies_of(t, part, sign, act):
        for m in INNER_MESSAGES if part else range(1, 19):
            at, inside = beside(LATTICE[m], sign)
            source, landing = message(t % 2, part, m)
            copy = pltpu.make_async_remote_copy(
                src_ref=source,
                dst_ref=landing,
                send_sem=send_sem.at[t, part, m - 1],
                recv_sem=recv_sem.at[t, part, m - 1],
                device_id=at,
                device_id_type=MESH,
            )

            @pl.when(inside)
            def _():
                act(copy)

    def send(t, part):
        copies_of(t, part, -1, lambda copy: copy.start())

    def sent(t, part):
        copies_of(t, part, -1, lambda copy: copy.wait_send())

    def receive(t, part):
        copies_of(t, part, 1, lambda copy: copy.wait_recv())

    def unpack_rows(b, part):
        for side in range(2):
            row = ROW0 + NY if side == 0 else ROW0 - 1
            for i, m in enumerate(Y_MEMBERS[side]):
                for k in range(2 * QUARTER):
                    x = QUARTER + k if part else k if k < QUARTER else NX - 2 * QUARTER + k
                    state[b][SLOT[m], x + 1, pl.ds(row, 1), :] = yrecv[b, part, side, i, pl.ds(k, 1), :]
        for m in range(15, 19):
            vector = LATTICE[m]
            side = 0 if vector[2] > 0 else 1
            row = ROW0 + NY if vector[1] > 0 else ROW0 - 1
            source = 0 if vector[1] > 0 else 7
            landing = zinner if part else zrecv
            landing[b, side, pl.ds(row, 1), :] = yzrecv[b, part, m - 15, pl.ds(source, 1), :]

    def unpack_outer(b):
        state[b][SLOT[9], NX + 1, pl.ds(ROW0, NY), :] = state[b][0, NX + 1, pl.ds(ROW0, NY), :]
        unpack_rows(b, 0)
        for m in range(7, 11):
            vector = LATTICE[m]
            plane_at = NX + 1 if vector[0] > 0 else 0
            row = ROW0 + NY if vector[1] > 0 else ROW0 - 1
            source = 0 if vector[0] > 0 else 7
            state[b][SLOT[m], plane_at, pl.ds(row, 1), :] = xyrecv[b, m - 7, pl.ds(source, 1), :]
        for m in range(11, 15):
            vector = LATTICE[m]
            side = 0 if vector[2] > 0 else 1
            i = Z_MEMBERS[side].index(m)
            source = i * LANES + (1 if vector[0] > 0 else NX)
            place = i * LANES + (NX + 1 if vector[0] > 0 else 0)
            for group in range(GROUPS):
                moved = pltpu.roll(
                    xzrecv[b, m - 11, pl.ds(8 * group, 8), :], (place - source) % NZ, 1
                )
                zrecv[b, side, rows_of(group), :] = jnp.where(
                    lane == place, moved, zrecv[b, side, rows_of(group), :]
                )

    in_plane = lax.rem(lane, LANES)
    inner_lane = (in_plane > QUARTER) & (in_plane <= NX - QUARTER)

    def unpack_inner(b):
        unpack_rows(b, 1)
        for side in range(2):
            for k in range(ROWS // 8):
                rows = pl.ds(8 * k, 8)
                zrecv[b, side, rows, :] = jnp.where(
                    inner_lane, zinner[b, side, rows, :], zrecv[b, side, rows, :]
                )

    send(0, 0)
    send(0, 1)
    loads[20].wait()
    loads[21].wait()

    def pull(b, x, group):
        read = []
        for m in range(19):
            vector = LATTICE[m]
            value = state[b][SLOT[m], x + 1 + vector[0], rows_of(group, vector[1]), :]
            if vector[2] != 0:
                side = 0 if vector[2] > 0 else 1
                place = Z_MEMBERS[side].index(m) * LANES + x + 1 + vector[0]
                column = zrecv[b, side, rows_of(group, vector[1]), :]
                if side == 0:
                    value = jnp.where(
                        lane == NZ - 1,
                        pltpu.roll(column, NZ - 1 - place, 1),
                        pltpu.roll(value, NZ - 1, 1),
                    )
                else:
                    value = jnp.where(
                        lane == 0,
                        pltpu.roll(column, NZ - place, 1),
                        pltpu.roll(value, 1, 1),
                    )
            read.append(value)
        return read

    def collide(read, u, is_solid):
        face_sum = [read[1] + read[2], read[3] + read[4], read[5] + read[6]]
        face_dif = [read[1] - read[2], read[3] - read[4], read[5] - read[6]]
        sums, twist, first, second = [], [], [], []
        for m in (7, 11, 15):
            plus, minus = read[m] + read[m + 1], read[m + 2] + read[m + 3]
            dplus, dminus = read[m] - read[m + 1], read[m + 2] - read[m + 3]
            sums.append(plus + minus)
            twist.append(plus - minus)
            first.append(dplus + dminus)
            second.append(dplus - dminus)
        xy, xz, yz = 0, 1, 2
        twice = [value + value for value in face_sum]
        rho = 12.0 * read[0] + (twice[0] + twice[1] + twice[2]) + (sums[xy] + sums[xz] + sums[yz])
        edge = [first[xy] + first[xz], second[xy] + first[yz], second[xz] + second[yz]]
        flux = [(face_dif[k] + face_dif[k]) + edge[k] for k in range(3)]
        stress = [
            twice[0] + (sums[xy] + sums[xz]),
            twice[1] + (sums[xy] + sums[yz]),
            twice[2] + (sums[xz] + sums[yz]),
        ]
        u3 = [3.0 * value for value in u]
        w = [
            rho * u[0] - (stress[0] * u3[0] + twist[xy] * u3[1] + twist[xz] * u3[2]),
            rho * u[1] - (twist[xy] * u3[0] + stress[1] * u3[1] + twist[yz] * u3[2]),
            rho * u[2] - (twist[xz] * u3[0] + twist[yz] * u3[1] + stress[2] * u3[2]),
        ]
        g = [(OMEGA * 3.0 / 36.0) * (flux[k] - w[k]) for k in range(3)]
        base = (OMEGA / 36.0) * rho + (OMEGA * 1.5 / 36.0) * (u[0] * w[0] + u[1] * w[1] + u[2] * w[2])
        along = [None] * 19
        along[0] = base
        for k in range(3):
            along[1 + 2 * k] = base + g[k]
            along[2 + 2 * k] = base - g[k]
        for m, (j, k) in ((7, (0, 1)), (11, (0, 2)), (15, (1, 2))):
            total, difference = g[j] + g[k], g[j] - g[k]
            along[m], along[m + 1] = base + total, base - total
            along[m + 2], along[m + 3] = base + difference, base - difference
        outputs = [
            jnp.where(is_solid, read[OPPOSITE[m]], along[m] + (1.0 - OMEGA) * read[m])
            for m in range(19)
        ]
        momentum = face_dif[2] + edge[2]
        pressure = jnp.where(is_solid, -momentum, 10.0 * g[2] + (1.0 - OMEGA) * momentum)
        return outputs, pressure

    out_row = lax.broadcasted_iota(jnp.int32, (128, NZ), 0)
    out_lane = lax.broadcasted_iota(jnp.int32, (128, NZ), 1)
    same_y = (out_row & 7) == (out_lane >> 4)
    own_lane = lax.broadcasted_iota(jnp.int32, (8, NZ), 0) == (lane >> 4)

    def one_step(t):
        b = t % 2
        nb = 1 - b
        last = t == STEPS - 1
        acc[...] = jnp.zeros_like(acc)
        receive(t, 0)
        unpack_outer(b)

        def one_plane(pair, high):
            x = NX - 1 - pair if high else pair
            for group in range(GROUPS):
                rows = pl.ds(8 * group, 8)
                read = pull(b, x, group)
                u = [vel[STEPS - 1 - t, k, x, rows, :] for k in range(3)]
                outputs, pressure = collide(read, u, solid[x, rows, :] == 1)
                for m in range(19):
                    if last:
                        out_ref[m, x, rows, :] = outputs[m]
                    else:
                        state[nb][SLOT[m], x + 1, rows_of(group), :] = outputs[m]
                if not last:
                    pack(nb, pair, high, group, outputs)
                upper = pressure.astype(jnp.bfloat16).astype(jnp.float32)
                both = jnp.concatenate([upper, pressure - upper], axis=0).astype(jnp.bfloat16)
                bits = (ids[x, rows, :] >> 4).astype(jnp.float32)
                bits = jnp.concatenate([bits, bits], axis=0).astype(jnp.bfloat16)
                for h in range(8):
                    hi_part[high, pl.ds(16 * h, 16), pl.ds(NZ * group, NZ)] = jnp.where(
                        bits == h, both, jnp.zeros_like(both)
                    )
            acc[...] += lax.dot_general(
                hi_part[high],
                lo_hot[x],
                (((1,), (1,)), ((), ())),
                preferred_element_type=jnp.float32,
            )

        def one_pair(pair, carry):
            @pl.when(pair == QUARTER - 1)
            def _():
                receive(t, 1)
                unpack_inner(b)

            if not last:

                @pl.when(pair == QUARTER)
                def _():
                    state[nb][0, 1, pl.ds(ROW0, NY), :] = state[nb][SLOT[9], 1, pl.ds(ROW0, NY), :]
                    send(t + 1, 0)

            one_plane(pair, 0)
            one_plane(pair, 1)
            return carry

        lax.fori_loop(0, PAIRS, one_pair, 0)
        if not last:
            send(t + 1, 1)
        sent(t, 0)
        sent(t, 1)

        own = jnp.where(same_y, acc[...], 0.0)
        total = jnp.sum(own.reshape(8, 16, NZ), axis=1)
        for shift in (64, 32, 16):
            total = total + pltpu.roll(total, shift, 1)
        sums[pl.ds(STEPS - 1 - t, 1), :] = jnp.sum(
            jnp.where(own_lane, total, 0.0), axis=0, keepdims=True
        )

    for t in range(STEPS):
        one_step(t)

    def gather_sum(own, slots, place, others, sems):
        slots[place] = own
        copies = []
        for k, target in enumerate(others):
            copies.append(
                pltpu.make_async_remote_copy(
                    src_ref=slots.at[place],
                    dst_ref=slots.at[place],
                    send_sem=sems.at[0, k],
                    recv_sem=sems.at[1, k],
                    device_id=target,
                    device_id_type=MESH,
                )
            )
        for copy in copies:
            copy.start()
        for copy in copies:
            copy.wait()
        total = slots[0]
        for k in range(1, len(others) + 1):
            total = total + slots[k]
        return total

    sums[pl.ds(STEPS, 8 - STEPS), :] = jnp.zeros((8 - STEPS, NZ), jnp.float32)
    total = gather_sum(sums[...], wall_xy, me[0] * sizes[1] + me[1], xy_others, xy_sem)
    total = gather_sum(total, wall_z, me[2], z_others, z_sem)
    cells_all = NX * NY * NZ * sizes[0] * sizes[1] * sizes[2]
    wall_ref[...] = total[:STEPS] * ((cells_all / (2.0 * WALLS)) ** (-0.5))


def body(terminal_adjoint, saved_velocity, solid_mask, wall_ids):
    sizes = tuple(lax.axis_size(name) for name in ("gx", "gy", "gz"))
    f32, vmem = jnp.float32, pltpu.VMEM
    return pl.pallas_call(
        functools.partial(kernel, sizes),
        out_shape=(
            pltpu.VMEM((19, NX, NY, NZ), f32),
            jax.ShapeDtypeStruct((STEPS, WALLS), f32),
        ),
        in_specs=[pl.BlockSpec(memory_space=pltpu.HBM)] * 4,
        out_specs=(pl.BlockSpec(memory_space=pltpu.VMEM),) * 2,
        scratch_shapes=[
            vmem((SLOTS, NX + 2, ROWS, NZ), f32),
            vmem((SLOTS, NX + 2, ROWS, NZ), f32),
            vmem((STEPS, 3, NX, NY, NZ), f32),
            vmem((NX, NY, NZ), jnp.int32),
            vmem((NX, NY, NZ), jnp.int32),
            vmem((2, 2, 2, 5, 2 * QUARTER, NZ), f32),
            vmem((2, 2, 2, 5, 2 * QUARTER, NZ), f32),
            vmem((2, 2, 2, NY, NZ), f32),
            vmem((2, 2, ROWS, NZ), f32),
            vmem((2, 2, ROWS, NZ), f32),
            vmem((2, 4, 8, NZ), f32),
            vmem((2, 4, NY, NZ), f32),
            vmem((2, 2, 4, 8, NZ), f32),
            vmem((NX, 128, GROUPS * NZ), jnp.bfloat16),
            vmem((2, 128, GROUPS * NZ), jnp.bfloat16),
            vmem((128, NZ), f32),
            vmem((8, NZ), f32),
            vmem((sizes[0] * sizes[1], 8, NZ), f32),
            vmem((sizes[2], 8, NZ), f32),
            pltpu.SemaphoreType.DMA((22,)),
            pltpu.SemaphoreType.DMA((STEPS, 2, 18)),
            pltpu.SemaphoreType.DMA((STEPS, 2, 18)),
            pltpu.SemaphoreType.DMA((2, max(1, sizes[0] * sizes[1] - 1))),
            pltpu.SemaphoreType.DMA((2, max(1, sizes[2] - 1))),
        ],
        compiler_params=pltpu.CompilerParams(
            collective_id=0, has_side_effects=True, vmem_limit_bytes=58 * 2**20
        ),
        name="adjoint_steps",
    )(terminal_adjoint, saved_velocity, solid_mask, wall_ids)


def solution(mesh):
    return jax.shard_map(
        body,
        mesh=mesh,
        in_specs=(
            P(None, "gx", "gy", "gz"),
            P(None, None, "gx", "gy", "gz"),
            P("gx", "gy", "gz"),
            P("gx", "gy", "gz"),
        ),
        out_specs=(P(None, "gx", "gy", "gz"), P()),
        check_vma=False,
    )
```

```python
import functools

import jax
import jax.numpy as jnp
from jax import lax
from jax.experimental import pallas as pl
from jax.experimental.pallas import tpu as pltpu
from jax.sharding import PartitionSpec as P

STEPS = 4
WALLS = 128
OMEGA = 1.25
LATTICE = (
    (0, 0, 0),
    (1, 0, 0),
    (-1, 0, 0),
    (0, 1, 0),
    (0, -1, 0),
    (0, 0, 1),
    (0, 0, -1),
    (1, 1, 0),
    (-1, -1, 0),
    (1, -1, 0),
    (-1, 1, 0),
    (1, 0, 1),
    (-1, 0, -1),
    (1, 0, -1),
    (-1, 0, 1),
    (0, 1, 1),
    (0, -1, -1),
    (0, 1, -1),
    (0, -1, 1),
)
OPPOSITE = (0, 2, 1, 4, 3, 6, 5, 8, 7, 10, 9, 12, 11, 14, 13, 16, 15, 18, 17)

NX, NY, NZ = 16, 32, 128
ROW0 = 8
ROWS = 48
GROUPS = NY // 8

SLOT = {9: 16, 1: 1, 11: 2, 13: 3, 7: 4, 3: 5, 15: 6, 17: 7, 10: 8, 2: 9,
        12: 10, 14: 11, 8: 12, 4: 13, 16: 14, 18: 15, 5: 17, 6: 18, 0: 19}
SLOTS = 20
Y_MEMBERS = ((7, 3, 15, 17, 10), (8, 4, 16, 18, 9))
Z_MEMBERS = ((5, 11, 14, 15, 18), (6, 12, 13, 16, 17))
LANES = NX + 2
PAIRS = NX // 2
PARTS = 2
SPAN = PAIRS // PARTS
INNER_MESSAGES = (3, 4, 5, 6, 15, 16, 17, 18)
MESH = pl.DeviceIdType.MESH


def kernel(
    sizes, adj_ref, vel_ref, solid_ref, ids_ref, out_ref, wall_ref,
    state0, state1, vel, solid, ids, ysend, yrecv, zsend, zrecv, zinner, xyrecv, xzrecv, yzrecv,
    lo_hot, hi_part, acc, sums, wall_xy, wall_z,
    in_sem, send_sem, recv_sem, xy_sem, z_sem,
):
    state = (state0, state1)
    me = (lax.axis_index("gx"), lax.axis_index("gy"), lax.axis_index("gz"))

    loads = []
    for m in range(19):
        loads.append(
            pltpu.make_async_copy(
                adj_ref.at[m],
                state[0].at[SLOT[m], pl.ds(1, NX), pl.ds(ROW0, NY), :],
                in_sem.at[m],
            )
        )
    loads.append(pltpu.make_async_copy(ids_ref, ids, in_sem.at[19]))
    loads.append(pltpu.make_async_copy(solid_ref, solid, in_sem.at[20]))
    loads.append(pltpu.make_async_copy(vel_ref, vel, in_sem.at[21]))
    for load in loads:
        load.start()

    for b in range(2):
        state[b][8:13, 0] = jnp.zeros((5, ROWS, NZ), jnp.float32)
        state[b][0:5, NX + 1] = jnp.zeros((5, ROWS, NZ), jnp.float32)
        state[b][SLOT[9], NX + 1] = jnp.zeros((ROWS, NZ), jnp.float32)
    yrecv[...] = jnp.zeros_like(yrecv)
    zrecv[...] = jnp.zeros_like(zrecv)
    zinner[...] = jnp.zeros_like(zinner)
    xyrecv[...] = jnp.zeros_like(xyrecv)
    xzrecv[...] = jnp.zeros_like(xzrecv)
    yzrecv[...] = jnp.zeros_like(yzrecv)

    def beside(vector, sign):
        at = tuple(me[k] + sign * vector[k] for k in range(3))
        inside = None
        for k in range(3):
            if vector[k] != 0:
                here = (at[k] >= 0) & (at[k] < sizes[k])
                inside = here if inside is None else inside & here
        return at, inside

    barrier = pltpu.get_barrier_semaphore()
    count = jnp.int32(0)
    for m in range(1, 19):
        at, inside = beside(LATTICE[m], 1)
        count = count + inside.astype(jnp.int32)

        @pl.when(inside)
        def _():
            pl.semaphore_signal(barrier, inc=1, device_id=at, device_id_type=MESH)

    plane = sizes[0] * sizes[1]
    xy_others, z_others = [], []
    for k in range(1, plane):
        there = lax.rem(me[0] * sizes[1] + me[1] + k, plane)
        xy_others.append((there // sizes[1], lax.rem(there, sizes[1]), me[2]))
    for k in range(1, sizes[2]):
        z_others.append((me[0], me[1], lax.rem(me[2] + k, sizes[2])))
    for target in xy_others + z_others:
        pl.semaphore_signal(barrier, inc=1, device_id=target, device_id_type=MESH)

    lane = lax.broadcasted_iota(jnp.int32, (8, NZ), 1)

    def rows_of(group, shift=0):
        return pl.ds(ROW0 + 8 * group + shift, 8)

    low_iota = lax.broadcasted_iota(jnp.int32, (16, NZ), 0)

    def hot_plane(x, carry):
        for group in range(GROUPS):
            low = ids[x, pl.ds(8 * group, 8), :] & 15
            for y in range(8):
                hot = jnp.broadcast_to(low[y : y + 1, :], (16, NZ)) == low_iota
                lo_hot[x, pl.ds(16 * y, 16), pl.ds(NZ * group, NZ)] = jnp.where(
                    hot, 1.0, 0.0
                ).astype(jnp.bfloat16)
        return carry


    def pack(b, pair, high, group, values):
        part = pair // SPAN
        x = NX - 1 - pair if high else pair
        row = lax.rem(pair, SPAN)
        row = 7 - row if high else row
        for side in range(2):
            rows = pl.ds(8 * group, 8)
            packed = zsend[b, part, side, rows, :]
            for i, m in enumerate(Z_MEMBERS[side]):
                place = i * LANES + x + 1
                moved = pltpu.roll(values[m], place + side, 1)
                packed = jnp.where(lane == place, moved, packed)
            zsend[b, part, side, rows, :] = packed
        if group == 0:
            for i, m in enumerate(Y_MEMBERS[0]):
                ysend[b, part, 0, i, pl.ds(row, 1), :] = values[m][0:1, :]
        if group == GROUPS - 1:
            for i, m in enumerate(Y_MEMBERS[1]):
                ysend[b, part, 1, i, pl.ds(row, 1), :] = values[m][7:8, :]


    def first_pack(pair, carry):
        for high in range(2):
            x = NX - 1 - pair if high else pair
            for group in range(GROUPS):
                values = {}
                for m in sorted(set(Y_MEMBERS[0] + Y_MEMBERS[1] + Z_MEMBERS[0] + Z_MEMBERS[1])):
                    values[m] = state[0][SLOT[m], x + 1, rows_of(group), :]
                pack(0, pair, high, group, values)
        return carry


    def message(b, part, m):
        cells = pl.ds(ROW0, NY)
        if m == 1:
            return state[b].at[pl.ds(0, 5), 1, cells, :], state[b].at[pl.ds(0, 5), NX + 1, cells, :]
        if m == 2:
            return state[b].at[pl.ds(8, 5), NX, cells, :], state[b].at[pl.ds(8, 5), 0, cells, :]
        if m in (3, 4):
            return ysend.at[b, part, m - 3], yrecv.at[b, part, m - 3]
        if m in (5, 6):
            landing = zinner.at[part - 1] if part else zrecv
            return zsend.at[b, part, m - 5], landing.at[b, m - 5, cells, :]
        vector = LATTICE[m]
        if m <= 10:
            side = 0 if vector[1] > 0 else 1
            return ysend.at[b, 0, side, Y_MEMBERS[side].index(m)], xyrecv.at[b, m - 7]
        side = 0 if vector[2] > 0 else 1
        if m <= 14:
            return zsend.at[b, 0, side], xzrecv.at[b, m - 11]
        start = 0 if vector[1] > 0 else NY - 8
        return zsend.at[b, part, side, pl.ds(start, 8), :], yzrecv.at[b, part, m - 15]

    def copies_of(t, part, sign, act):
        for m in INNER_MESSAGES if part else range(1, 19):
            at, inside = beside(LATTICE[m], sign)
            source, landing = message(t % 2, part, m)
            copy = pltpu.make_async_remote_copy(
                src_ref=source,
                dst_ref=landing,
                send_sem=send_sem.at[t, part, m - 1],
                recv_sem=recv_sem.at[t, part, m - 1],
                device_id=at,
                device_id_type=MESH,
            )

            @pl.when(inside)
            def _():
                act(copy)

    def send(t, part):
        copies_of(t, part, -1, lambda copy: copy.start())

    def sent(t, part):
        copies_of(t, part, -1, lambda copy: copy.wait_send())

    def receive(t, part):
        copies_of(t, part, 1, lambda copy: copy.wait_recv())

    def unpack_rows(b, part):
        for side in range(2):
            row = ROW0 + NY if side == 0 else ROW0 - 1
            for i, m in enumerate(Y_MEMBERS[side]):
                for k in range(SPAN):
                    pair = part * SPAN + k
                    for x, source in ((pair, k), (NX - 1 - pair, 7 - k)):
                        state[b][SLOT[m], x + 1, pl.ds(row, 1), :] = yrecv[
                            b, part, side, i, pl.ds(source, 1), :
                        ]
        for m in range(15, 19):
            vector = LATTICE[m]
            side = 0 if vector[2] > 0 else 1
            row = ROW0 + NY if vector[1] > 0 else ROW0 - 1
            source = 0 if vector[1] > 0 else 7
            landing = zinner.at[part - 1] if part else zrecv
            landing[b, side, pl.ds(row, 1), :] = yzrecv[b, part, m - 15, pl.ds(source, 1), :]

    def unpack_outer(b):
        state[b][SLOT[9], NX + 1, pl.ds(ROW0, NY), :] = state[b][0, NX + 1, pl.ds(ROW0, NY), :]
        unpack_rows(b, 0)
        for m in range(7, 11):
            vector = LATTICE[m]
            plane_at = NX + 1 if vector[0] > 0 else 0
            row = ROW0 + NY if vector[1] > 0 else ROW0 - 1
            source = 0 if vector[0] > 0 else 7
            state[b][SLOT[m], plane_at, pl.ds(row, 1), :] = xyrecv[b, m - 7, pl.ds(source, 1), :]
        for m in range(11, 15):
            vector = LATTICE[m]
            side = 0 if vector[2] > 0 else 1
            i = Z_MEMBERS[side].index(m)
            source = i * LANES + (1 if vector[0] > 0 else NX)
            place = i * LANES + (NX + 1 if vector[0] > 0 else 0)
            for group in range(GROUPS):
                moved = pltpu.roll(
                    xzrecv[b, m - 11, pl.ds(8 * group, 8), :], (place - source) % NZ, 1
                )
                zrecv[b, side, rows_of(group), :] = jnp.where(
                    lane == place, moved, zrecv[b, side, rows_of(group), :]
                )

    in_plane = lax.rem(lane, LANES)

    def unpack_inner(b, part):
        inner_lane = (in_plane > part * SPAN) & (in_plane <= NX - part * SPAN)
        unpack_rows(b, part)
        for side in range(2):
            for k in range(ROWS // 8):
                rows = pl.ds(8 * k, 8)
                zrecv[b, side, rows, :] = jnp.where(
                    inner_lane, zinner[part - 1, b, side, rows, :], zrecv[b, side, rows, :]
                )

    for m in range(19):
        loads[m].wait()
    pl.semaphore_wait(barrier, count + len(xy_others) + len(z_others))
    for part in range(PARTS):
        lax.fori_loop(part * SPAN, (part + 1) * SPAN, first_pack, 0)
        if part == 0:
            state[0][0, 1, pl.ds(ROW0, NY), :] = state[0][SLOT[9], 1, pl.ds(ROW0, NY), :]
        send(0, part)
    loads[19].wait()
    lax.fori_loop(0, NX, hot_plane, 0)
    loads[20].wait()
    loads[21].wait()

    def pull(b, x, group):
        read = []
        for m in range(19):
            vector = LATTICE[m]
            value = state[b][SLOT[m], x + 1 + vector[0], rows_of(group, vector[1]), :]
            if vector[2] != 0:
                side = 0 if vector[2] > 0 else 1
                place = Z_MEMBERS[side].index(m) * LANES + x + 1 + vector[0]
                column = zrecv[b, side, rows_of(group, vector[1]), :]
                if side == 0:
                    value = jnp.where(
                        lane == NZ - 1,
                        pltpu.roll(column, NZ - 1 - place, 1),
                        pltpu.roll(value, NZ - 1, 1),
                    )
                else:
                    value = jnp.where(
                        lane == 0,
                        pltpu.roll(column, NZ - place, 1),
                        pltpu.roll(value, 1, 1),
                    )
            read.append(value)
        return read

    def collide(read, u, is_solid):
        face_sum = [read[1] + read[2], read[3] + read[4], read[5] + read[6]]
        face_dif = [read[1] - read[2], read[3] - read[4], read[5] - read[6]]
        sums, twist, first, second = [], [], [], []
        for m in (7, 11, 15):
            plus, minus = read[m] + read[m + 1], read[m + 2] + read[m + 3]
            dplus, dminus = read[m] - read[m + 1], read[m + 2] - read[m + 3]
            sums.append(plus + minus)
            twist.append(plus - minus)
            first.append(dplus + dminus)
            second.append(dplus - dminus)
        xy, xz, yz = 0, 1, 2
        twice = [value + value for value in face_sum]
        rho = 12.0 * read[0] + (twice[0] + twice[1] + twice[2]) + (sums[xy] + sums[xz] + sums[yz])
        edge = [first[xy] + first[xz], second[xy] + first[yz], second[xz] + second[yz]]
        flux = [(face_dif[k] + face_dif[k]) + edge[k] for k in range(3)]
        stress = [
            twice[0] + (sums[xy] + sums[xz]),
            twice[1] + (sums[xy] + sums[yz]),
            twice[2] + (sums[xz] + sums[yz]),
        ]
        u3 = [3.0 * value for value in u]
        w = [
            rho * u[0] - (stress[0] * u3[0] + twist[xy] * u3[1] + twist[xz] * u3[2]),
            rho * u[1] - (twist[xy] * u3[0] + stress[1] * u3[1] + twist[yz] * u3[2]),
            rho * u[2] - (twist[xz] * u3[0] + twist[yz] * u3[1] + stress[2] * u3[2]),
        ]
        g = [(OMEGA * 3.0 / 36.0) * (flux[k] - w[k]) for k in range(3)]
        base = (OMEGA / 36.0) * rho + (OMEGA * 1.5 / 36.0) * (u[0] * w[0] + u[1] * w[1] + u[2] * w[2])
        along = [None] * 19
        along[0] = base
        for k in range(3):
            along[1 + 2 * k] = base + g[k]
            along[2 + 2 * k] = base - g[k]
        for m, (j, k) in ((7, (0, 1)), (11, (0, 2)), (15, (1, 2))):
            total, difference = g[j] + g[k], g[j] - g[k]
            along[m], along[m + 1] = base + total, base - total
            along[m + 2], along[m + 3] = base + difference, base - difference
        outputs = [
            jnp.where(is_solid, read[OPPOSITE[m]], along[m] + (1.0 - OMEGA) * read[m])
            for m in range(19)
        ]
        momentum = face_dif[2] + edge[2]
        pressure = jnp.where(is_solid, -momentum, 10.0 * g[2] + (1.0 - OMEGA) * momentum)
        return outputs, pressure

    out_row = lax.broadcasted_iota(jnp.int32, (128, NZ), 0)
    out_lane = lax.broadcasted_iota(jnp.int32, (128, NZ), 1)
    same_y = (out_row & 7) == (out_lane >> 4)
    own_lane = lax.broadcasted_iota(jnp.int32, (8, NZ), 0) == (lane >> 4)

    def one_step(t):
        b = t % 2
        nb = 1 - b
        last = t == STEPS - 1
        acc[...] = jnp.zeros_like(acc)
        receive(t, 0)
        unpack_outer(b)

        def one_plane(pair, high):
            x = NX - 1 - pair if high else pair
            for group in range(GROUPS):
                rows = pl.ds(8 * group, 8)
                read = pull(b, x, group)
                u = [vel[STEPS - 1 - t, k, x, rows, :] for k in range(3)]
                outputs, pressure = collide(read, u, solid[x, rows, :] == 1)
                for m in range(19):
                    if last:
                        out_ref[m, x, rows, :] = outputs[m]
                    else:
                        state[nb][SLOT[m], x + 1, rows_of(group), :] = outputs[m]
                if not last:
                    pack(nb, pair, high, group, outputs)
                upper = pressure.astype(jnp.bfloat16).astype(jnp.float32)
                both = jnp.concatenate([upper, pressure - upper], axis=0).astype(jnp.bfloat16)
                bits = (ids[x, rows, :] >> 4).astype(jnp.float32)
                bits = jnp.concatenate([bits, bits], axis=0).astype(jnp.bfloat16)
                for h in range(8):
                    hi_part[high, pl.ds(16 * h, 16), pl.ds(NZ * group, NZ)] = jnp.where(
                        bits == h, both, jnp.zeros_like(both)
                    )
            acc[...] += lax.dot_general(
                hi_part[high],
                lo_hot[x],
                (((1,), (1,)), ((), ())),
                preferred_element_type=jnp.float32,
            )

        def one_pair(pair, carry):
            for part in range(1, PARTS):

                @pl.when(pair == part * SPAN - 1)
                def _():
                    receive(t, part)
                    unpack_inner(b, part)

                if not last:

                    @pl.when(pair == part * SPAN)
                    def _():
                        if part == 1:
                            cells = pl.ds(ROW0, NY)
                            state[nb][0, 1, cells, :] = state[nb][SLOT[9], 1, cells, :]
                        send(t + 1, part - 1)

            one_plane(pair, 0)
            one_plane(pair, 1)
            return carry

        lax.fori_loop(0, PAIRS, one_pair, 0)
        if not last:
            send(t + 1, PARTS - 1)
        for part in range(PARTS):
            sent(t, part)

        own = jnp.where(same_y, acc[...], 0.0)
        total = jnp.sum(own.reshape(8, 16, NZ), axis=1)
        for shift in (64, 32, 16):
            total = total + pltpu.roll(total, shift, 1)
        sums[pl.ds(STEPS - 1 - t, 1), :] = jnp.sum(
            jnp.where(own_lane, total, 0.0), axis=0, keepdims=True
        )

    for t in range(STEPS):
        one_step(t)

    def gather_sum(own, slots, place, others, sems):
        slots[place] = own
        copies = []
        for k, target in enumerate(others):
            copies.append(
                pltpu.make_async_remote_copy(
                    src_ref=slots.at[place],
                    dst_ref=slots.at[place],
                    send_sem=sems.at[0, k],
                    recv_sem=sems.at[1, k],
                    device_id=target,
                    device_id_type=MESH,
                )
            )
        for copy in copies:
            copy.start()
        for copy in copies:
            copy.wait()
        total = slots[0]
        for k in range(1, len(others) + 1):
            total = total + slots[k]
        return total

    sums[pl.ds(STEPS, 8 - STEPS), :] = jnp.zeros((8 - STEPS, NZ), jnp.float32)
    total = gather_sum(sums[...], wall_xy, me[0] * sizes[1] + me[1], xy_others, xy_sem)
    total = gather_sum(total, wall_z, me[2], z_others, z_sem)
    cells_all = NX * NY * NZ * sizes[0] * sizes[1] * sizes[2]
    wall_ref[...] = total[:STEPS] * ((cells_all / (2.0 * WALLS)) ** (-0.5))


def body(terminal_adjoint, saved_velocity, solid_mask, wall_ids):
    sizes = tuple(lax.axis_size(name) for name in ("gx", "gy", "gz"))
    f32, vmem = jnp.float32, pltpu.VMEM
    return pl.pallas_call(
        functools.partial(kernel, sizes),
        out_shape=(
            pltpu.VMEM((19, NX, NY, NZ), f32),
            jax.ShapeDtypeStruct((STEPS, WALLS), f32),
        ),
        in_specs=[pl.BlockSpec(memory_space=pltpu.HBM)] * 4,
        out_specs=(pl.BlockSpec(memory_space=pltpu.VMEM),) * 2,
        scratch_shapes=[
            vmem((SLOTS, NX + 2, ROWS, NZ), f32),
            vmem((SLOTS, NX + 2, ROWS, NZ), f32),
            vmem((STEPS, 3, NX, NY, NZ), f32),
            vmem((NX, NY, NZ), jnp.int32),
            vmem((NX, NY, NZ), jnp.int32),
            vmem((2, PARTS, 2, 5, 8, NZ), f32),
            vmem((2, PARTS, 2, 5, 8, NZ), f32),
            vmem((2, PARTS, 2, NY, NZ), f32),
            vmem((2, 2, ROWS, NZ), f32),
            vmem((PARTS - 1, 2, 2, ROWS, NZ), f32),
            vmem((2, 4, 8, NZ), f32),
            vmem((2, 4, NY, NZ), f32),
            vmem((2, PARTS, 4, 8, NZ), f32),
            vmem((NX, 128, GROUPS * NZ), jnp.bfloat16),
            vmem((2, 128, GROUPS * NZ), jnp.bfloat16),
            vmem((128, NZ), f32),
            vmem((8, NZ), f32),
            vmem((sizes[0] * sizes[1], 8, NZ), f32),
            vmem((sizes[2], 8, NZ), f32),
            pltpu.SemaphoreType.DMA((22,)),
            pltpu.SemaphoreType.DMA((STEPS, PARTS, 18)),
            pltpu.SemaphoreType.DMA((STEPS, PARTS, 18)),
            pltpu.SemaphoreType.DMA((2, max(1, sizes[0] * sizes[1] - 1))),
            pltpu.SemaphoreType.DMA((2, max(1, sizes[2] - 1))),
        ],
        compiler_params=pltpu.CompilerParams(
            collective_id=0, has_side_effects=True, vmem_limit_bytes=58 * 2**20
        ),
        name="adjoint_steps",
    )(terminal_adjoint, saved_velocity, solid_mask, wall_ids)


def solution(mesh):
    return jax.shard_map(
        body,
        mesh=mesh,
        in_specs=(
            P(None, "gx", "gy", "gz"),
            P(None, None, "gx", "gy", "gz"),
            P("gx", "gy", "gz"),
            P("gx", "gy", "gz"),
        ),
        out_specs=(P(None, "gx", "gy", "gz"), P()),
        check_vma=False,
    )
```

```python
import functools

import jax
import jax.numpy as jnp
from jax import lax
from jax.experimental import pallas as pl
from jax.experimental.pallas import tpu as pltpu
from jax.sharding import PartitionSpec as P

STEPS = 4
WALLS = 128
OMEGA = 1.25
LATTICE = (
    (0, 0, 0),
    (1, 0, 0),
    (-1, 0, 0),
    (0, 1, 0),
    (0, -1, 0),
    (0, 0, 1),
    (0, 0, -1),
    (1, 1, 0),
    (-1, -1, 0),
    (1, -1, 0),
    (-1, 1, 0),
    (1, 0, 1),
    (-1, 0, -1),
    (1, 0, -1),
    (-1, 0, 1),
    (0, 1, 1),
    (0, -1, -1),
    (0, 1, -1),
    (0, -1, 1),
)
OPPOSITE = (0, 2, 1, 4, 3, 6, 5, 8, 7, 10, 9, 12, 11, 14, 13, 16, 15, 18, 17)

NX, NY, NZ = 16, 32, 128
ROW0 = 8
ROWS = 48
GROUPS = NY // 8

SLOT = {9: 16, 1: 1, 11: 2, 13: 3, 7: 4, 3: 5, 15: 6, 17: 7, 10: 8, 2: 9,
        12: 10, 14: 11, 8: 12, 4: 13, 16: 14, 18: 15, 5: 17, 6: 18, 0: 19}
SLOTS = 20
Y_MEMBERS = ((7, 3, 15, 17, 10), (8, 4, 16, 18, 9))
Z_MEMBERS = ((5, 11, 14, 15, 18), (6, 12, 13, 16, 17))
LANES = NX + 2
PAIRS = NX // 2
PARTS = 2
SPAN = PAIRS // PARTS
ACROSS = PARTS
ALONG_MESSAGES = (3, 4, 5, 6, 15, 16, 17, 18)
ACROSS_MESSAGES = (1, 2, 7, 8, 9, 10, 11, 12, 13, 14)
MESH = pl.DeviceIdType.MESH


def kernel(
    sizes, adj_ref, vel_ref, solid_ref, ids_ref, out_ref, wall_ref,
    state0, state1, vel, solid, ids, ysend, yrecv, zsend, zrecv, zinner, xyrecv, xzrecv, yzrecv,
    lo_hot, hi_part, acc, sums, wall_xy, wall_z,
    in_sem, send_sem, recv_sem, xy_sem, z_sem,
):
    state = (state0, state1)
    me = (lax.axis_index("gx"), lax.axis_index("gy"), lax.axis_index("gz"))

    loads = []
    for m in range(19):
        loads.append(
            pltpu.make_async_copy(
                adj_ref.at[m],
                state[0].at[SLOT[m], pl.ds(1, NX), pl.ds(ROW0, NY), :],
                in_sem.at[m],
            )
        )
    loads.append(pltpu.make_async_copy(ids_ref, ids, in_sem.at[19]))
    loads.append(pltpu.make_async_copy(solid_ref, solid, in_sem.at[20]))
    loads.append(pltpu.make_async_copy(vel_ref, vel, in_sem.at[21]))
    for load in loads:
        load.start()

    for b in range(2):
        state[b][8:13, 0] = jnp.zeros((5, ROWS, NZ), jnp.float32)
        state[b][0:5, NX + 1] = jnp.zeros((5, ROWS, NZ), jnp.float32)
        state[b][SLOT[9], NX + 1] = jnp.zeros((ROWS, NZ), jnp.float32)
    yrecv[...] = jnp.zeros_like(yrecv)
    zrecv[...] = jnp.zeros_like(zrecv)
    zinner[...] = jnp.zeros_like(zinner)
    xyrecv[...] = jnp.zeros_like(xyrecv)
    xzrecv[...] = jnp.zeros_like(xzrecv)
    yzrecv[...] = jnp.zeros_like(yzrecv)

    def beside(vector, sign):
        at = tuple(me[k] + sign * vector[k] for k in range(3))
        inside = None
        for k in range(3):
            if vector[k] != 0:
                here = (at[k] >= 0) & (at[k] < sizes[k])
                inside = here if inside is None else inside & here
        return at, inside

    barrier = pltpu.get_barrier_semaphore()
    count = jnp.int32(0)
    for m in range(1, 19):
        at, inside = beside(LATTICE[m], 1)
        count = count + inside.astype(jnp.int32)

        @pl.when(inside)
        def _():
            pl.semaphore_signal(barrier, inc=1, device_id=at, device_id_type=MESH)

    plane = sizes[0] * sizes[1]
    xy_others, z_others = [], []
    for k in range(1, plane):
        there = lax.rem(me[0] * sizes[1] + me[1] + k, plane)
        xy_others.append((there // sizes[1], lax.rem(there, sizes[1]), me[2]))
    for k in range(1, sizes[2]):
        z_others.append((me[0], me[1], lax.rem(me[2] + k, sizes[2])))
    for target in xy_others + z_others:
        pl.semaphore_signal(barrier, inc=1, device_id=target, device_id_type=MESH)

    lane = lax.broadcasted_iota(jnp.int32, (8, NZ), 1)

    def rows_of(group, shift=0):
        return pl.ds(ROW0 + 8 * group + shift, 8)

    low_iota = lax.broadcasted_iota(jnp.int32, (16, NZ), 0)

    def hot_plane(x, carry):
        for group in range(GROUPS):
            low = ids[x, pl.ds(8 * group, 8), :] & 15
            for y in range(8):
                hot = jnp.broadcast_to(low[y : y + 1, :], (16, NZ)) == low_iota
                lo_hot[x, pl.ds(16 * y, 16), pl.ds(NZ * group, NZ)] = jnp.where(
                    hot, 1.0, 0.0
                ).astype(jnp.bfloat16)
        return carry


    def pack(b, pair, high, group, values):
        part = pair // SPAN
        x = NX - 1 - pair if high else pair
        row = lax.rem(pair, SPAN)
        row = 7 - row if high else row
        for side in range(2):
            rows = pl.ds(8 * group, 8)
            packed = zsend[b, part, side, rows, :]
            for i, m in enumerate(Z_MEMBERS[side]):
                place = i * LANES + x + 1
                moved = pltpu.roll(values[m], place + side, 1)
                packed = jnp.where(lane == place, moved, packed)
            zsend[b, part, side, rows, :] = packed
        if group == 0:
            for i, m in enumerate(Y_MEMBERS[0]):
                ysend[b, part, 0, i, pl.ds(row, 1), :] = values[m][0:1, :]
        if group == GROUPS - 1:
            for i, m in enumerate(Y_MEMBERS[1]):
                ysend[b, part, 1, i, pl.ds(row, 1), :] = values[m][7:8, :]


    def first_pack(pair, carry):
        for high in range(2):
            x = NX - 1 - pair if high else pair
            for group in range(GROUPS):
                values = {}
                for m in sorted(set(Y_MEMBERS[0] + Y_MEMBERS[1] + Z_MEMBERS[0] + Z_MEMBERS[1])):
                    values[m] = state[0][SLOT[m], x + 1, rows_of(group), :]
                pack(0, pair, high, group, values)
        return carry


    def message(b, part, m):
        cells = pl.ds(ROW0, NY)
        if m == 1:
            return state[b].at[pl.ds(0, 5), 1, cells, :], state[b].at[pl.ds(0, 5), NX + 1, cells, :]
        if m == 2:
            return state[b].at[pl.ds(8, 5), NX, cells, :], state[b].at[pl.ds(8, 5), 0, cells, :]
        if m in (3, 4):
            return ysend.at[b, part, m - 3], yrecv.at[b, part, m - 3]
        if m in (5, 6):
            landing = zinner.at[part - 1] if part else zrecv
            return zsend.at[b, part, m - 5], landing.at[b, m - 5, cells, :]
        vector = LATTICE[m]
        if m <= 10:
            side = 0 if vector[1] > 0 else 1
            return ysend.at[b, 0, side, Y_MEMBERS[side].index(m)], xyrecv.at[b, m - 7]
        side = 0 if vector[2] > 0 else 1
        if m <= 14:
            return zsend.at[b, 0, side], xzrecv.at[b, m - 11]
        start = 0 if vector[1] > 0 else NY - 8
        return zsend.at[b, part, side, pl.ds(start, 8), :], yzrecv.at[b, part, m - 15]

    def copies_of(t, part, sign, act):
        for m in ACROSS_MESSAGES if part == ACROSS else ALONG_MESSAGES:
            at, inside = beside(LATTICE[m], sign)
            source, landing = message(t % 2, part, m)
            copy = pltpu.make_async_remote_copy(
                src_ref=source,
                dst_ref=landing,
                send_sem=send_sem.at[t, part, m - 1],
                recv_sem=recv_sem.at[t, part, m - 1],
                device_id=at,
                device_id_type=MESH,
            )

            @pl.when(inside)
            def _():
                act(copy)

    def send(t, part):
        copies_of(t, part, -1, lambda copy: copy.start())

    def sent(t, part):
        copies_of(t, part, -1, lambda copy: copy.wait_send())

    def receive(t, part):
        copies_of(t, part, 1, lambda copy: copy.wait_recv())

    def unpack_rows(b, part):
        for side in range(2):
            row = ROW0 + NY if side == 0 else ROW0 - 1
            for i, m in enumerate(Y_MEMBERS[side]):
                for k in range(SPAN):
                    pair = part * SPAN + k
                    for x, source in ((pair, k), (NX - 1 - pair, 7 - k)):
                        state[b][SLOT[m], x + 1, pl.ds(row, 1), :] = yrecv[
                            b, part, side, i, pl.ds(source, 1), :
                        ]
        for m in range(15, 19):
            vector = LATTICE[m]
            side = 0 if vector[2] > 0 else 1
            row = ROW0 + NY if vector[1] > 0 else ROW0 - 1
            source = 0 if vector[1] > 0 else 7
            landing = zinner.at[part - 1] if part else zrecv
            landing[b, side, pl.ds(row, 1), :] = yzrecv[b, part, m - 15, pl.ds(source, 1), :]

    def unpack_across(b):
        state[b][SLOT[9], NX + 1, pl.ds(ROW0, NY), :] = state[b][0, NX + 1, pl.ds(ROW0, NY), :]
        for m in range(7, 11):
            vector = LATTICE[m]
            plane_at = NX + 1 if vector[0] > 0 else 0
            row = ROW0 + NY if vector[1] > 0 else ROW0 - 1
            source = 0 if vector[0] > 0 else 7
            state[b][SLOT[m], plane_at, pl.ds(row, 1), :] = xyrecv[b, m - 7, pl.ds(source, 1), :]
        for m in range(11, 15):
            vector = LATTICE[m]
            side = 0 if vector[2] > 0 else 1
            i = Z_MEMBERS[side].index(m)
            source = i * LANES + (1 if vector[0] > 0 else NX)
            place = i * LANES + (NX + 1 if vector[0] > 0 else 0)
            for group in range(GROUPS):
                moved = pltpu.roll(
                    xzrecv[b, m - 11, pl.ds(8 * group, 8), :], (place - source) % NZ, 1
                )
                zrecv[b, side, rows_of(group), :] = jnp.where(
                    lane == place, moved, zrecv[b, side, rows_of(group), :]
                )

    in_plane = lax.rem(lane, LANES)

    def unpack_inner(b, part):
        inner_lane = (in_plane > part * SPAN) & (in_plane <= NX - part * SPAN)
        unpack_rows(b, part)
        for side in range(2):
            for k in range(ROWS // 8):
                rows = pl.ds(8 * k, 8)
                zrecv[b, side, rows, :] = jnp.where(
                    inner_lane, zinner[part - 1, b, side, rows, :], zrecv[b, side, rows, :]
                )

    for m in range(19):
        loads[m].wait()
    pl.semaphore_wait(barrier, count + len(xy_others) + len(z_others))
    for part in range(PARTS):
        lax.fori_loop(part * SPAN, (part + 1) * SPAN, first_pack, 0)
        if part == 0:
            state[0][0, 1, pl.ds(ROW0, NY), :] = state[0][SLOT[9], 1, pl.ds(ROW0, NY), :]
        send(0, part)
        if part == 0:
            send(0, ACROSS)
    loads[19].wait()
    lax.fori_loop(0, NX, hot_plane, 0)
    loads[20].wait()
    loads[21].wait()

    def pull(b, x, group):
        read = []
        for m in range(19):
            vector = LATTICE[m]
            value = state[b][SLOT[m], x + 1 + vector[0], rows_of(group, vector[1]), :]
            if vector[2] != 0:
                side = 0 if vector[2] > 0 else 1
                place = Z_MEMBERS[side].index(m) * LANES + x + 1 + vector[0]
                column = zrecv[b, side, rows_of(group, vector[1]), :]
                if side == 0:
                    value = jnp.where(
                        lane == NZ - 1,
                        pltpu.roll(column, NZ - 1 - place, 1),
                        pltpu.roll(value, NZ - 1, 1),
                    )
                else:
                    value = jnp.where(
                        lane == 0,
                        pltpu.roll(column, NZ - place, 1),
                        pltpu.roll(value, 1, 1),
                    )
            read.append(value)
        return read

    def collide(read, u, is_solid):
        face_sum = [read[1] + read[2], read[3] + read[4], read[5] + read[6]]
        face_dif = [read[1] - read[2], read[3] - read[4], read[5] - read[6]]
        sums, twist, first, second = [], [], [], []
        for m in (7, 11, 15):
            plus, minus = read[m] + read[m + 1], read[m + 2] + read[m + 3]
            dplus, dminus = read[m] - read[m + 1], read[m + 2] - read[m + 3]
            sums.append(plus + minus)
            twist.append(plus - minus)
            first.append(dplus + dminus)
            second.append(dplus - dminus)
        xy, xz, yz = 0, 1, 2
        twice = [value + value for value in face_sum]
        rho = 12.0 * read[0] + (twice[0] + twice[1] + twice[2]) + (sums[xy] + sums[xz] + sums[yz])
        edge = [first[xy] + first[xz], second[xy] + first[yz], second[xz] + second[yz]]
        flux = [(face_dif[k] + face_dif[k]) + edge[k] for k in range(3)]
        stress = [
            twice[0] + (sums[xy] + sums[xz]),
            twice[1] + (sums[xy] + sums[yz]),
            twice[2] + (sums[xz] + sums[yz]),
        ]
        u3 = [3.0 * value for value in u]
        w = [
            rho * u[0] - (stress[0] * u3[0] + twist[xy] * u3[1] + twist[xz] * u3[2]),
            rho * u[1] - (twist[xy] * u3[0] + stress[1] * u3[1] + twist[yz] * u3[2]),
            rho * u[2] - (twist[xz] * u3[0] + twist[yz] * u3[1] + stress[2] * u3[2]),
        ]
        g = [(OMEGA * 3.0 / 36.0) * (flux[k] - w[k]) for k in range(3)]
        base = (OMEGA / 36.0) * rho + (OMEGA * 1.5 / 36.0) * (u[0] * w[0] + u[1] * w[1] + u[2] * w[2])
        along = [None] * 19
        along[0] = base
        for k in range(3):
            along[1 + 2 * k] = base + g[k]
            along[2 + 2 * k] = base - g[k]
        for m, (j, k) in ((7, (0, 1)), (11, (0, 2)), (15, (1, 2))):
            total, difference = g[j] + g[k], g[j] - g[k]
            along[m], along[m + 1] = base + total, base - total
            along[m + 2], along[m + 3] = base + difference, base - difference
        outputs = [
            jnp.where(is_solid, read[OPPOSITE[m]], along[m] + (1.0 - OMEGA) * read[m])
            for m in range(19)
        ]
        momentum = face_dif[2] + edge[2]
        pressure = jnp.where(is_solid, -momentum, 10.0 * g[2] + (1.0 - OMEGA) * momentum)
        return outputs, pressure

    out_row = lax.broadcasted_iota(jnp.int32, (128, NZ), 0)
    out_lane = lax.broadcasted_iota(jnp.int32, (128, NZ), 1)
    same_y = (out_row & 7) == (out_lane >> 4)
    own_lane = lax.broadcasted_iota(jnp.int32, (8, NZ), 0) == (lane >> 4)

    def one_step(t):
        b = t % 2
        nb = 1 - b
        last = t == STEPS - 1
        acc[...] = jnp.zeros_like(acc)
        receive(t, 0)
        unpack_rows(b, 0)

        def one_plane(pair, high):
            x = NX - 1 - pair if high else pair
            for group in range(GROUPS):
                rows = pl.ds(8 * group, 8)
                read = pull(b, x, group)
                u = [vel[STEPS - 1 - t, k, x, rows, :] for k in range(3)]
                outputs, pressure = collide(read, u, solid[x, rows, :] == 1)
                for m in range(19):
                    if last:
                        out_ref[m, x, rows, :] = outputs[m]
                    else:
                        state[nb][SLOT[m], x + 1, rows_of(group), :] = outputs[m]
                if not last:
                    pack(nb, pair, high, group, outputs)
                upper = pressure.astype(jnp.bfloat16).astype(jnp.float32)
                both = jnp.concatenate([upper, pressure - upper], axis=0).astype(jnp.bfloat16)
                bits = (ids[x, rows, :] >> 4).astype(jnp.float32)
                bits = jnp.concatenate([bits, bits], axis=0).astype(jnp.bfloat16)
                for h in range(8):
                    hi_part[high, pl.ds(16 * h, 16), pl.ds(NZ * group, NZ)] = jnp.where(
                        bits == h, both, jnp.zeros_like(both)
                    )
            acc[...] += lax.dot_general(
                hi_part[high],
                lo_hot[x],
                (((1,), (1,)), ((), ())),
                preferred_element_type=jnp.float32,
            )

        def one_pair(i, carry):
            later = lax.div(i + PAIRS - 3, PAIRS)
            pair = later * i + (1 - later) * lax.rem(i + 1, 3)

            @pl.when(i == 2)
            def _():
                receive(t, ACROSS)
                unpack_across(b)

            for part in range(1, PARTS):

                @pl.when(i == part * SPAN - 1)
                def _():
                    receive(t, part)
                    unpack_inner(b, part)

                if not last:

                    @pl.when(i == part * SPAN)
                    def _():
                        if part == 1:
                            cells = pl.ds(ROW0, NY)
                            state[nb][0, 1, cells, :] = state[nb][SLOT[9], 1, cells, :]
                        send(t + 1, part - 1)
                        if part == 1:
                            send(t + 1, ACROSS)

            one_plane(pair, 0)
            one_plane(pair, 1)
            return carry

        lax.fori_loop(0, PAIRS, one_pair, 0)
        if not last:
            send(t + 1, PARTS - 1)
        for part in range(PARTS + 1):
            sent(t, part)

        own = jnp.where(same_y, acc[...], 0.0)
        total = jnp.sum(own.reshape(8, 16, NZ), axis=1)
        for shift in (64, 32, 16):
            total = total + pltpu.roll(total, shift, 1)
        sums[pl.ds(STEPS - 1 - t, 1), :] = jnp.sum(
            jnp.where(own_lane, total, 0.0), axis=0, keepdims=True
        )

    for t in range(STEPS):
        one_step(t)

    def gather_sum(own, slots, place, others, sems):
        slots[place] = own
        copies = []
        for k, target in enumerate(others):
            copies.append(
                pltpu.make_async_remote_copy(
                    src_ref=slots.at[place],
                    dst_ref=slots.at[place],
                    send_sem=sems.at[0, k],
                    recv_sem=sems.at[1, k],
                    device_id=target,
                    device_id_type=MESH,
                )
            )
        for copy in copies:
            copy.start()
        for copy in copies:
            copy.wait()
        total = slots[0]
        for k in range(1, len(others) + 1):
            total = total + slots[k]
        return total

    sums[pl.ds(STEPS, 8 - STEPS), :] = jnp.zeros((8 - STEPS, NZ), jnp.float32)
    total = gather_sum(sums[...], wall_xy, me[0] * sizes[1] + me[1], xy_others, xy_sem)
    total = gather_sum(total, wall_z, me[2], z_others, z_sem)
    cells_all = NX * NY * NZ * sizes[0] * sizes[1] * sizes[2]
    wall_ref[...] = total[:STEPS] * ((cells_all / (2.0 * WALLS)) ** (-0.5))


def body(terminal_adjoint, saved_velocity, solid_mask, wall_ids):
    sizes = tuple(lax.axis_size(name) for name in ("gx", "gy", "gz"))
    f32, vmem = jnp.float32, pltpu.VMEM
    return pl.pallas_call(
        functools.partial(kernel, sizes),
        out_shape=(
            pltpu.VMEM((19, NX, NY, NZ), f32),
            jax.ShapeDtypeStruct((STEPS, WALLS), f32),
        ),
        in_specs=[pl.BlockSpec(memory_space=pltpu.HBM)] * 4,
        out_specs=(pl.BlockSpec(memory_space=pltpu.VMEM),) * 2,
        scratch_shapes=[
            vmem((SLOTS, NX + 2, ROWS, NZ), f32),
            vmem((SLOTS, NX + 2, ROWS, NZ), f32),
            vmem((STEPS, 3, NX, NY, NZ), f32),
            vmem((NX, NY, NZ), jnp.int32),
            vmem((NX, NY, NZ), jnp.int32),
            vmem((2, PARTS, 2, 5, 8, NZ), f32),
            vmem((2, PARTS, 2, 5, 8, NZ), f32),
            vmem((2, PARTS, 2, NY, NZ), f32),
            vmem((2, 2, ROWS, NZ), f32),
            vmem((PARTS - 1, 2, 2, ROWS, NZ), f32),
            vmem((2, 4, 8, NZ), f32),
            vmem((2, 4, NY, NZ), f32),
            vmem((2, PARTS, 4, 8, NZ), f32),
            vmem((NX, 128, GROUPS * NZ), jnp.bfloat16),
            vmem((2, 128, GROUPS * NZ), jnp.bfloat16),
            vmem((128, NZ), f32),
            vmem((8, NZ), f32),
            vmem((sizes[0] * sizes[1], 8, NZ), f32),
            vmem((sizes[2], 8, NZ), f32),
            pltpu.SemaphoreType.DMA((22,)),
            pltpu.SemaphoreType.DMA((STEPS, PARTS + 1, 18)),
            pltpu.SemaphoreType.DMA((STEPS, PARTS + 1, 18)),
            pltpu.SemaphoreType.DMA((2, max(1, sizes[0] * sizes[1] - 1))),
            pltpu.SemaphoreType.DMA((2, max(1, sizes[2] - 1))),
        ],
        compiler_params=pltpu.CompilerParams(
            collective_id=0, has_side_effects=True, vmem_limit_bytes=58 * 2**20
        ),
        name="adjoint_steps",
    )(terminal_adjoint, saved_velocity, solid_mask, wall_ids)


def solution(mesh):
    return jax.shard_map(
        body,
        mesh=mesh,
        in_specs=(
            P(None, "gx", "gy", "gz"),
            P(None, None, "gx", "gy", "gz"),
            P("gx", "gy", "gz"),
            P("gx", "gy", "gz"),
        ),
        out_specs=(P(None, "gx", "gy", "gz"), P()),
        check_vma=False,
    )
```

```python
import functools

import jax
import jax.numpy as jnp
from jax import lax
from jax.experimental import pallas as pl
from jax.experimental.pallas import tpu as pltpu
from jax.sharding import PartitionSpec as P

STEPS = 4
WALLS = 128
OMEGA = 1.25
LATTICE = (
    (0, 0, 0),
    (1, 0, 0),
    (-1, 0, 0),
    (0, 1, 0),
    (0, -1, 0),
    (0, 0, 1),
    (0, 0, -1),
    (1, 1, 0),
    (-1, -1, 0),
    (1, -1, 0),
    (-1, 1, 0),
    (1, 0, 1),
    (-1, 0, -1),
    (1, 0, -1),
    (-1, 0, 1),
    (0, 1, 1),
    (0, -1, -1),
    (0, 1, -1),
    (0, -1, 1),
)
OPPOSITE = (0, 2, 1, 4, 3, 6, 5, 8, 7, 10, 9, 12, 11, 14, 13, 16, 15, 18, 17)

NX, NY, NZ = 16, 32, 128
ROW0 = 8
ROWS = 48
GROUPS = NY // 8

SLOT = {9: 16, 1: 1, 11: 2, 13: 3, 7: 4, 3: 5, 15: 6, 17: 7, 10: 8, 2: 9,
        12: 10, 14: 11, 8: 12, 4: 13, 16: 14, 18: 15, 5: 17, 6: 18, 0: 19}
SLOTS = 20
Y_MEMBERS = ((7, 3, 15, 17, 10), (8, 4, 16, 18, 9))
Z_MEMBERS = ((5, 11, 14, 15, 18), (6, 12, 13, 16, 17))
LANES = NX + 2
PAIRS = NX // 2
PARTS = 2
SPAN = PAIRS // PARTS
ACROSS = PARTS
ALONG_MESSAGES = (3, 4, 5, 6, 15, 16, 17, 18)
ACROSS_MESSAGES = (1, 2, 7, 8, 9, 10, 11, 12, 13, 14)
MESH = pl.DeviceIdType.MESH


def kernel(
    sizes, adj_ref, vel_ref, solid_ref, ids_ref, out_ref, wall_ref,
    state0, state1, vel, solid, ids, ysend, yrecv, zsend, zrecv, zinner, xyrecv, xzrecv, yzrecv,
    lo_hot, hi_part, acc, sums, wall_xy, wall_z,
    in_sem, send_sem, recv_sem, xy_sem, z_sem,
):
    state = (state0, state1)
    me = (lax.axis_index("gx"), lax.axis_index("gy"), lax.axis_index("gz"))

    loads = []
    for m in range(19):
        loads.append(
            pltpu.make_async_copy(
                adj_ref.at[m],
                state[0].at[SLOT[m], pl.ds(1, NX), pl.ds(ROW0, NY), :],
                in_sem.at[m],
            )
        )
    loads.append(pltpu.make_async_copy(ids_ref, ids, in_sem.at[19]))
    loads.append(pltpu.make_async_copy(solid_ref, solid, in_sem.at[20]))
    loads.append(pltpu.make_async_copy(vel_ref, vel, in_sem.at[21]))
    for load in loads:
        load.start()

    for b in range(2):
        state[b][8:13, 0] = jnp.zeros((5, ROWS, NZ), jnp.float32)
        state[b][0:5, NX + 1] = jnp.zeros((5, ROWS, NZ), jnp.float32)
        state[b][SLOT[9], NX + 1] = jnp.zeros((ROWS, NZ), jnp.float32)
    yrecv[...] = jnp.zeros_like(yrecv)
    zrecv[...] = jnp.zeros_like(zrecv)
    zinner[...] = jnp.zeros_like(zinner)
    xyrecv[...] = jnp.zeros_like(xyrecv)
    xzrecv[...] = jnp.zeros_like(xzrecv)
    yzrecv[...] = jnp.zeros_like(yzrecv)

    def beside(vector, sign):
        at = tuple(me[k] + sign * vector[k] for k in range(3))
        inside = None
        for k in range(3):
            if vector[k] != 0:
                here = (at[k] >= 0) & (at[k] < sizes[k])
                inside = here if inside is None else inside & here
        return at, inside

    barrier = pltpu.get_barrier_semaphore()
    count = jnp.int32(0)
    for m in range(1, 19):
        at, inside = beside(LATTICE[m], 1)
        count = count + inside.astype(jnp.int32)

        @pl.when(inside)
        def _():
            pl.semaphore_signal(barrier, inc=1, device_id=at, device_id_type=MESH)

    plane = sizes[0] * sizes[1]
    xy_others, z_others = [], []
    for k in range(1, plane):
        there = lax.rem(me[0] * sizes[1] + me[1] + k, plane)
        xy_others.append((there // sizes[1], lax.rem(there, sizes[1]), me[2]))
    for k in range(1, sizes[2]):
        z_others.append((me[0], me[1], lax.rem(me[2] + k, sizes[2])))
    for target in xy_others + z_others:
        pl.semaphore_signal(barrier, inc=1, device_id=target, device_id_type=MESH)

    lane = lax.broadcasted_iota(jnp.int32, (8, NZ), 1)

    def rows_of(group, shift=0):
        return pl.ds(ROW0 + 8 * group + shift, 8)

    low_iota = lax.broadcasted_iota(jnp.int32, (16, NZ), 0)

    def hot_plane(x, carry):
        for group in range(GROUPS):
            low = ids[x, pl.ds(8 * group, 8), :] & 15
            for y in range(8):
                hot = jnp.broadcast_to(low[y : y + 1, :], (16, NZ)) == low_iota
                lo_hot[x, pl.ds(16 * y, 16), pl.ds(NZ * group, NZ)] = jnp.where(
                    hot, 1.0, 0.0
                ).astype(jnp.bfloat16)
        return carry


    def pack(b, pair, high, group, values):
        part = pair // SPAN
        x = NX - 1 - pair if high else pair
        row = lax.rem(pair, SPAN)
        row = 7 - row if high else row
        for side in range(2):
            rows = pl.ds(8 * group, 8)
            packed = zsend[b, part, side, rows, :]
            for i, m in enumerate(Z_MEMBERS[side]):
                place = i * LANES + x + 1
                moved = pltpu.roll(values[m], place + side, 1)
                packed = jnp.where(lane == place, moved, packed)
            zsend[b, part, side, rows, :] = packed
        if group == 0:
            for i, m in enumerate(Y_MEMBERS[0]):
                ysend[b, part, 0, i, pl.ds(row, 1), :] = values[m][0:1, :]
        if group == GROUPS - 1:
            for i, m in enumerate(Y_MEMBERS[1]):
                ysend[b, part, 1, i, pl.ds(row, 1), :] = values[m][7:8, :]


    def first_pack(pair, carry):
        for high in range(2):
            x = NX - 1 - pair if high else pair
            for group in range(GROUPS):
                values = {}
                for m in sorted(set(Y_MEMBERS[0] + Y_MEMBERS[1] + Z_MEMBERS[0] + Z_MEMBERS[1])):
                    values[m] = state[0][SLOT[m], x + 1, rows_of(group), :]
                pack(0, pair, high, group, values)
        return carry


    def message(b, part, m):
        cells = pl.ds(ROW0, NY)
        if m == 1:
            return state[b].at[pl.ds(0, 5), 1, cells, :], state[b].at[pl.ds(0, 5), NX + 1, cells, :]
        if m == 2:
            return state[b].at[pl.ds(8, 5), NX, cells, :], state[b].at[pl.ds(8, 5), 0, cells, :]
        if m in (3, 4):
            return ysend.at[b, part, m - 3], yrecv.at[b, part, m - 3]
        if m in (5, 6):
            landing = zinner.at[part - 1] if part else zrecv
            return zsend.at[b, part, m - 5], landing.at[b, m - 5, cells, :]
        vector = LATTICE[m]
        if m <= 10:
            side = 0 if vector[1] > 0 else 1
            return ysend.at[b, 0, side, Y_MEMBERS[side].index(m)], xyrecv.at[b, m - 7]
        side = 0 if vector[2] > 0 else 1
        if m <= 14:
            return zsend.at[b, 0, side], xzrecv.at[b, m - 11]
        start = 0 if vector[1] > 0 else NY - 8
        return zsend.at[b, part, side, pl.ds(start, 8), :], yzrecv.at[b, part, m - 15]

    def copies_of(t, part, sign, act):
        for m in ACROSS_MESSAGES if part == ACROSS else ALONG_MESSAGES:
            at, inside = beside(LATTICE[m], sign)
            source, landing = message(t % 2, part, m)
            copy = pltpu.make_async_remote_copy(
                src_ref=source,
                dst_ref=landing,
                send_sem=send_sem.at[t, part, m - 1],
                recv_sem=recv_sem.at[t, part, m - 1],
                device_id=at,
                device_id_type=MESH,
            )

            @pl.when(inside)
            def _():
                act(copy)

    def send(t, part):
        copies_of(t, part, -1, lambda copy: copy.start())

    def sent(t, part):
        copies_of(t, part, -1, lambda copy: copy.wait_send())

    def receive(t, part):
        copies_of(t, part, 1, lambda copy: copy.wait_recv())

    def unpack_rows(b, part):
        for side in range(2):
            row = ROW0 + NY if side == 0 else ROW0 - 1
            for i, m in enumerate(Y_MEMBERS[side]):
                for k in range(SPAN):
                    pair = part * SPAN + k
                    for x, source in ((pair, k), (NX - 1 - pair, 7 - k)):
                        state[b][SLOT[m], x + 1, pl.ds(row, 1), :] = yrecv[
                            b, part, side, i, pl.ds(source, 1), :
                        ]
        for m in range(15, 19):
            vector = LATTICE[m]
            side = 0 if vector[2] > 0 else 1
            row = ROW0 + NY if vector[1] > 0 else ROW0 - 1
            source = 0 if vector[1] > 0 else 7
            landing = zinner.at[part - 1] if part else zrecv
            landing[b, side, pl.ds(row, 1), :] = yzrecv[b, part, m - 15, pl.ds(source, 1), :]

    def unpack_across(b):
        state[b][SLOT[9], NX + 1, pl.ds(ROW0, NY), :] = state[b][0, NX + 1, pl.ds(ROW0, NY), :]
        for m in range(7, 11):
            vector = LATTICE[m]
            plane_at = NX + 1 if vector[0] > 0 else 0
            row = ROW0 + NY if vector[1] > 0 else ROW0 - 1
            source = 0 if vector[0] > 0 else 7
            state[b][SLOT[m], plane_at, pl.ds(row, 1), :] = xyrecv[b, m - 7, pl.ds(source, 1), :]
        for m in range(11, 15):
            vector = LATTICE[m]
            side = 0 if vector[2] > 0 else 1
            i = Z_MEMBERS[side].index(m)
            source = i * LANES + (1 if vector[0] > 0 else NX)
            place = i * LANES + (NX + 1 if vector[0] > 0 else 0)
            for group in range(GROUPS):
                moved = pltpu.roll(
                    xzrecv[b, m - 11, pl.ds(8 * group, 8), :], (place - source) % NZ, 1
                )
                zrecv[b, side, rows_of(group), :] = jnp.where(
                    lane == place, moved, zrecv[b, side, rows_of(group), :]
                )

    in_plane = lax.rem(lane, LANES)

    def unpack_inner(b, part):
        inner_lane = (in_plane > part * SPAN) & (in_plane <= NX - part * SPAN)
        unpack_rows(b, part)
        for side in range(2):
            for k in range(ROWS // 8):
                rows = pl.ds(8 * k, 8)
                zrecv[b, side, rows, :] = jnp.where(
                    inner_lane, zinner[part - 1, b, side, rows, :], zrecv[b, side, rows, :]
                )

    for m in range(19):
        loads[m].wait()
    pl.semaphore_wait(barrier, count + len(xy_others) + len(z_others))
    for part in range(PARTS):
        lax.fori_loop(part * SPAN, (part + 1) * SPAN, first_pack, 0)
        if part == 0:
            state[0][0, 1, pl.ds(ROW0, NY), :] = state[0][SLOT[9], 1, pl.ds(ROW0, NY), :]
        send(0, part)
        if part == 0:
            send(0, ACROSS)
    loads[19].wait()
    lax.fori_loop(0, NX, hot_plane, 0)
    loads[20].wait()
    loads[21].wait()

    def pull(b, x, group):
        read = []
        for m in range(19):
            vector = LATTICE[m]
            value = state[b][SLOT[m], x + 1 + vector[0], rows_of(group, vector[1]), :]
            if vector[2] != 0:
                side = 0 if vector[2] > 0 else 1
                place = Z_MEMBERS[side].index(m) * LANES + x + 1 + vector[0]
                column = zrecv[b, side, rows_of(group, vector[1]), :]
                if side == 0:
                    value = jnp.where(
                        lane == NZ - 1,
                        pltpu.roll(column, NZ - 1 - place, 1),
                        pltpu.roll(value, NZ - 1, 1),
                    )
                else:
                    value = jnp.where(
                        lane == 0,
                        pltpu.roll(column, NZ - place, 1),
                        pltpu.roll(value, 1, 1),
                    )
            read.append(value)
        return read

    def collide(read, u, is_solid):
        face_sum = [read[1] + read[2], read[3] + read[4], read[5] + read[6]]
        face_dif = [read[1] - read[2], read[3] - read[4], read[5] - read[6]]
        sums, twist, first, second = [], [], [], []
        for m in (7, 11, 15):
            plus, minus = read[m] + read[m + 1], read[m + 2] + read[m + 3]
            dplus, dminus = read[m] - read[m + 1], read[m + 2] - read[m + 3]
            sums.append(plus + minus)
            twist.append(plus - minus)
            first.append(dplus + dminus)
            second.append(dplus - dminus)
        xy, xz, yz = 0, 1, 2
        twice = [value + value for value in face_sum]
        rho = 12.0 * read[0] + (twice[0] + twice[1] + twice[2]) + (sums[xy] + sums[xz] + sums[yz])
        edge = [first[xy] + first[xz], second[xy] + first[yz], second[xz] + second[yz]]
        flux = [(face_dif[k] + face_dif[k]) + edge[k] for k in range(3)]
        stress = [
            twice[0] + (sums[xy] + sums[xz]),
            twice[1] + (sums[xy] + sums[yz]),
            twice[2] + (sums[xz] + sums[yz]),
        ]
        u3 = [3.0 * value for value in u]
        w = [
            rho * u[0] - (stress[0] * u3[0] + twist[xy] * u3[1] + twist[xz] * u3[2]),
            rho * u[1] - (twist[xy] * u3[0] + stress[1] * u3[1] + twist[yz] * u3[2]),
            rho * u[2] - (twist[xz] * u3[0] + twist[yz] * u3[1] + stress[2] * u3[2]),
        ]
        g = [(OMEGA * 3.0 / 36.0) * (flux[k] - w[k]) for k in range(3)]
        base = (OMEGA / 36.0) * rho + (OMEGA * 1.5 / 36.0) * (u[0] * w[0] + u[1] * w[1] + u[2] * w[2])
        along = [None] * 19
        along[0] = base
        for k in range(3):
            along[1 + 2 * k] = base + g[k]
            along[2 + 2 * k] = base - g[k]
        for m, (j, k) in ((7, (0, 1)), (11, (0, 2)), (15, (1, 2))):
            total, difference = g[j] + g[k], g[j] - g[k]
            along[m], along[m + 1] = base + total, base - total
            along[m + 2], along[m + 3] = base + difference, base - difference
        outputs = [
            jnp.where(is_solid, read[OPPOSITE[m]], along[m] + (1.0 - OMEGA) * read[m])
            for m in range(19)
        ]
        momentum = face_dif[2] + edge[2]
        pressure = jnp.where(is_solid, -momentum, 10.0 * g[2] + (1.0 - OMEGA) * momentum)
        return outputs, pressure

    out_row = lax.broadcasted_iota(jnp.int32, (128, NZ), 0)
    out_lane = lax.broadcasted_iota(jnp.int32, (128, NZ), 1)
    same_y = (out_row & 7) == (out_lane >> 4)
    own_lane = lax.broadcasted_iota(jnp.int32, (8, NZ), 0) == (lane >> 4)

    def one_step(t):
        b = t % 2
        nb = 1 - b
        last = t == STEPS - 1
        acc[...] = jnp.zeros_like(acc)
        receive(t, 0)
        unpack_rows(b, 0)

        def one_plane(pair, high):
            x = NX - 1 - pair if high else pair
            for group in range(GROUPS):
                rows = pl.ds(8 * group, 8)
                read = pull(b, x, group)
                u = [vel[STEPS - 1 - t, k, x, rows, :] for k in range(3)]
                outputs, pressure = collide(read, u, solid[x, rows, :] == 1)
                for m in range(19):
                    if last:
                        out_ref[m, x, rows, :] = outputs[m]
                    else:
                        state[nb][SLOT[m], x + 1, rows_of(group), :] = outputs[m]
                if not last:
                    pack(nb, pair, high, group, outputs)
                upper = pressure.astype(jnp.bfloat16).astype(jnp.float32)
                both = jnp.concatenate([upper, pressure - upper], axis=0).astype(jnp.bfloat16)
                bits = (ids[x, rows, :] >> 4).astype(jnp.float32)
                bits = jnp.concatenate([bits, bits], axis=0).astype(jnp.bfloat16)
                for h in range(8):
                    hi_part[high, pl.ds(16 * h, 16), pl.ds(NZ * group, NZ)] = jnp.where(
                        bits == h, both, jnp.zeros_like(both)
                    )
            acc[...] += lax.dot_general(
                hi_part[high],
                lo_hot[x],
                (((1,), (1,)), ((), ())),
                preferred_element_type=jnp.float32,
            )

        def one_pair(i, carry):
            later = lax.div(i + PAIRS - 3, PAIRS)
            pair = later * i + (1 - later) * lax.rem(i + 1, 3)

            @pl.when(i == 2)
            def _():
                receive(t, ACROSS)
                unpack_across(b)

            for part in range(1, PARTS):

                @pl.when(i == part * SPAN - 1)
                def _():
                    receive(t, part)
                    unpack_inner(b, part)

                if not last:

                    @pl.when(i == part * SPAN)
                    def _():
                        if part == 1:
                            cells = pl.ds(ROW0, NY)
                            state[nb][0, 1, cells, :] = state[nb][SLOT[9], 1, cells, :]
                        send(t + 1, part - 1)
                        if part == 1:
                            send(t + 1, ACROSS)

            one_plane(pair, 0)
            one_plane(pair, 1)
            return carry

        lax.fori_loop(0, PAIRS, one_pair, 0)
        if not last:
            send(t + 1, PARTS - 1)
        for part in range(PARTS + 1):
            sent(t, part)

        own = jnp.where(same_y, acc[...], 0.0)
        total = jnp.sum(own.reshape(8, 16, NZ), axis=1)
        for shift in (64, 32, 16):
            total = total + pltpu.roll(total, shift, 1)
        sums[pl.ds(STEPS - 1 - t, 1), :] = jnp.sum(
            jnp.where(own_lane, total, 0.0), axis=0, keepdims=True
        )

    for t in range(STEPS):
        one_step(t)

    def gather_sum(own, slots, place, others, sems):
        slots[place] = own
        copies = []
        for k, target in enumerate(others):
            copies.append(
                pltpu.make_async_remote_copy(
                    src_ref=slots.at[place],
                    dst_ref=slots.at[place],
                    send_sem=sems.at[0, k],
                    recv_sem=sems.at[1, k],
                    device_id=target,
                    device_id_type=MESH,
                )
            )
        for copy in copies:
            copy.start()
        for copy in copies:
            copy.wait()
        total = slots[0]
        for k in range(1, len(others) + 1):
            total = total + slots[k]
        return total

    sums[pl.ds(STEPS, 8 - STEPS), :] = jnp.zeros((8 - STEPS, NZ), jnp.float32)
    total = gather_sum(sums[...], wall_xy, me[0] * sizes[1] + me[1], xy_others, xy_sem)
    total = gather_sum(total, wall_z, me[2], z_others, z_sem)
    cells_all = NX * NY * NZ * sizes[0] * sizes[1] * sizes[2]
    wall_ref[...] = total[:STEPS] * ((cells_all / (2.0 * WALLS)) ** (-0.5))


def body(terminal_adjoint, saved_velocity, solid_mask, wall_ids):
    sizes = tuple(lax.axis_size(name) for name in ("gx", "gy", "gz"))
    f32, vmem = jnp.float32, pltpu.VMEM
    return pl.pallas_call(
        functools.partial(kernel, sizes),
        out_shape=(
            pltpu.VMEM((19, NX, NY, NZ), f32),
            pltpu.VMEM((STEPS, WALLS), f32),
        ),
        in_specs=[pl.BlockSpec(memory_space=pltpu.HBM)] * 4,
        out_specs=(pl.BlockSpec(memory_space=pltpu.VMEM),) * 2,
        scratch_shapes=[
            vmem((SLOTS, NX + 2, ROWS, NZ), f32),
            vmem((SLOTS, NX + 2, ROWS, NZ), f32),
            vmem((STEPS, 3, NX, NY, NZ), f32),
            vmem((NX, NY, NZ), jnp.int32),
            vmem((NX, NY, NZ), jnp.int32),
            vmem((2, PARTS, 2, 5, 8, NZ), f32),
            vmem((2, PARTS, 2, 5, 8, NZ), f32),
            vmem((2, PARTS, 2, NY, NZ), f32),
            vmem((2, 2, ROWS, NZ), f32),
            vmem((PARTS - 1, 2, 2, ROWS, NZ), f32),
            vmem((2, 4, 8, NZ), f32),
            vmem((2, 4, NY, NZ), f32),
            vmem((2, PARTS, 4, 8, NZ), f32),
            vmem((NX, 128, GROUPS * NZ), jnp.bfloat16),
            vmem((2, 128, GROUPS * NZ), jnp.bfloat16),
            vmem((128, NZ), f32),
            vmem((8, NZ), f32),
            vmem((sizes[0] * sizes[1], 8, NZ), f32),
            vmem((sizes[2], 8, NZ), f32),
            pltpu.SemaphoreType.DMA((22,)),
            pltpu.SemaphoreType.DMA((STEPS, PARTS + 1, 18)),
            pltpu.SemaphoreType.DMA((STEPS, PARTS + 1, 18)),
            pltpu.SemaphoreType.DMA((2, max(1, sizes[0] * sizes[1] - 1))),
            pltpu.SemaphoreType.DMA((2, max(1, sizes[2] - 1))),
        ],
        compiler_params=pltpu.CompilerParams(
            collective_id=0, has_side_effects=True, vmem_limit_bytes=58 * 2**20
        ),
        name="adjoint_steps",
    )(terminal_adjoint, saved_velocity, solid_mask, wall_ids)


def solution(mesh):
    return jax.shard_map(
        body,
        mesh=mesh,
        in_specs=(
            P(None, "gx", "gy", "gz"),
            P(None, None, "gx", "gy", "gz"),
            P("gx", "gy", "gz"),
            P("gx", "gy", "gz"),
        ),
        out_specs=(P(None, "gx", "gy", "gz"), P()),
        check_vma=False,
    )
```
